768 devices in a mesh: dom: 48 (over z, x), feat: 16 (over y, core).
Axes of the slice: x: 4, y: 8, z: 12, core: 2. Of those that a mesh axis runs over, the one named last changes fastest.
Arguments:
- features: float32 [256, 98304], P('feat', 'dom'), may hold values from -6 to 6
- tile_vals: float32 [768, 6, 128, 128], P(('dom', 'feat')), may hold values from -0.21875 to 0.21875
- tile_src: int32 [768, 6], P(('dom', 'feat')), may hold values from 0 to 33, as said below
- tile_count: int32 [768], P(('dom', 'feat')), may hold values from 3 to 6, as said below
- send_rows: int32 [2304, 32], P('dom'), may hold values from 0 to 2047
- hub_owner: int32 [768], replicated, may hold values from 0 to 47, as said below
- hub_row: int32 [768], replicated, may hold values from 0 to 2047
- weight: float32 [256, 256], P(None, 'feat'), may hold values from -0.375 to 0.375
- cotangent: float32 [256, 98304], P(None, ('dom', 'feat')), may hold values from -0.01953125 to 0.01953125
Outputs:
- output: float32 [256, 98304], P(None, ('dom', 'feat'))
- grad_weight: float32 [256, 256], P(None, 'feat')
The draws below stay inside these ranges and needn't reach their ends.
Inputs may be any that keep to these rules, and one draw needn't show every extreme that they name: `tile_src`: slot 0 of destination tile t of a partition names that partition's own tile t, slot 1 a boundary tile (indices 16 up to the first hub tile), slot 2 a hub tile (the last ones); other slots any source tile. `tile_count`: some partition has all its destination tiles at 6 live slots. `hub_owner`: each partition owns at most 48 hub vertices, and some partition owns exactly 48.
All inputs are finite; a program needn't handle non-finite values.
Results may differ from the reference program's by a relative error of at most 0.0003.
Values sent between devices are 32-bit elements; how exact they have to be, the bound alone decides.
A program may use at most 32 MiB of HBM per device.

```python
import jax
import jax.numpy as jnp
from jax import lax

D = 256
NODE_DEV = 2048
TILE = 128
SLOTS = 6
SEND = 32
HUB_MOST = 48
NODES = 98304
NODE_TILES = 16
HUBS = 768
EXT_TILES = 34
N_DOM = 48


def draw_tile_src(key, part):
    key = jax.random.fold_in(key, 11)
    first_key, second_key, third_key = jax.random.split(key, 3)
    row_count = N_DOM * NODE_TILES
    border_tiles = N_DOM * SEND // TILE
    own_tiles = jnp.arange(row_count, dtype=jnp.int32) % NODE_TILES
    border_tile = NODE_TILES + jax.random.randint(first_key, (row_count,), 0, border_tiles)
    hub_tile = NODE_TILES + border_tiles + jax.random.randint(second_key, (row_count,), 0, HUBS // TILE)
    others = jax.random.randint(third_key, (row_count, SLOTS - 3), 0, EXT_TILES)
    return jnp.concatenate([own_tiles[:, None], border_tile[:, None], hub_tile[:, None], others], axis=1).astype(jnp.int32)


def draw_tile_count(key, part):
    key = jax.random.fold_in(key, 23)
    first_key, second_key, third_key = jax.random.split(key, 3)
    row_count = N_DOM * NODE_TILES
    device_cap = jax.random.randint(first_key, (N_DOM,), 3, SLOTS + 1)
    device_of = jnp.arange(row_count, dtype=jnp.int32) // NODE_TILES
    spread = jax.random.randint(second_key, (row_count,), 0, 65536)
    counts = 3 + spread % (device_cap[device_of] - 2)
    fullest = jax.random.randint(third_key, (), 0, N_DOM)
    return jnp.where(device_of == fullest, SLOTS, counts).astype(jnp.int32)


def draw_hub_owner(key, part):
    key = jax.random.fold_in(key, 37)
    first_key, second_key, third_key = jax.random.split(key, 3)
    slot_total = N_DOM * HUB_MOST
    owners = jnp.arange(slot_total, dtype=jnp.int32) // HUB_MOST
    levels = jax.random.randint(first_key, (N_DOM,), 0, 4)
    divisor = jnp.array([1, 2, 4, 8], dtype=jnp.int32)[levels]
    forced = jax.random.randint(second_key, (), 0, N_DOM)
    base_score = jax.random.randint(third_key, (slot_total,), 0, 4096) // divisor[owners]
    scores = base_score + jnp.where(owners == forced, 4096, 0)
    distinct = scores * slot_total + jnp.arange(slot_total, dtype=jnp.int32)
    unused, chosen = lax.top_k(distinct, HUBS)
    return owners[chosen].astype(jnp.int32)


def with_ends(result, own_key, smallest, largest):
    dims = result.shape
    place = [jax.random.randint(jax.random.fold_in(own_key, axis), (), 0, dims[axis]) for axis in range(len(dims))]
    result = result.at[tuple(place)].set(smallest)
    longest = dims.index(max(dims))
    place[longest] = (place[longest] + 1) % dims[longest]
    return result.at[tuple(place)].set(largest)


def shard_levels(own_key, dims, cuts, low, largest):
    def one(axis_at, parts):
        draws = jax.random.uniform(jax.random.fold_in(jax.random.fold_in(own_key, 6), axis_at), (parts,), jnp.float32, low / len(cuts), largest / len(cuts))
        return jnp.repeat(jnp.exp(draws), dims[axis_at] // parts).reshape((-1,) + (1,) * (len(dims) - axis_at - 1))

    level = one(*cuts[0])
    for cut in cuts[1:]:
        level = level * one(*cut)
    return level


def bell_draw(rng, extent, scale, limit, shards=(), held_as=jnp.bfloat16):
    values = jax.random.normal(rng, extent, jnp.float32) * scale
    if len(shards) > 0:
        values = shard_levels(rng, extent, shards, -0.22, 0.18) * values
    return jnp.clip(values, min=-limit, max=limit).astype(held_as)


def setup_inputs(seed: int = 0) -> dict:
    key_of = jax.random.split(jax.random.key(seed), 10)
    features = bell_draw(key_of[0], (D, NODES), 1.0, 6.0, ((0, 16), (1, 48)), jnp.float32)
    tile_vals = bell_draw(key_of[1], (N_DOM * NODE_DEV // TILE, SLOTS, TILE, TILE), (TILE * SLOTS) ** -0.5, 0.21875, ((0, 768),), jnp.float32)
    tile_src = draw_tile_src(jax.random.fold_in(key_of[9], 71), 0)
    tile_count = draw_tile_count(jax.random.fold_in(key_of[9], 71), 0)
    send_rows = with_ends(jax.random.randint(key_of[4], (N_DOM * N_DOM, SEND), 0, NODE_DEV), jax.random.fold_in(key_of[4], 1), 0, NODE_DEV - 1).astype(jnp.int32)
    hub_owner = draw_hub_owner(jax.random.fold_in(key_of[9], 71), 0)
    hub_row = with_ends(jax.random.randint(key_of[6], (HUBS,), 0, NODE_DEV), jax.random.fold_in(key_of[6], 1), 0, NODE_DEV - 1).astype(jnp.int32)
    weight = bell_draw(key_of[7], (D, D), D ** -0.5, 0.375, ((1, 16),), jnp.float32)
    cotangent = bell_draw(key_of[8], (D, NODES), NODES ** -0.5, 0.01953125, ((1, 768),), jnp.float32)
    return {"features": features, "tile_vals": tile_vals, "tile_src": tile_src, "tile_count": tile_count, "send_rows": send_rows, "hub_owner": hub_owner, "hub_row": hub_row, "weight": weight, "cotangent": cotangent}


def reference(features, tile_vals, tile_src, tile_count, send_rows, hub_owner, hub_row, weight, cotangent):
    partitions = features.reshape(D, N_DOM, NODE_DEV)
    hub_block = partitions[:, hub_owner, hub_row]
    incoming = send_rows.reshape(N_DOM, N_DOM, SEND).transpose(1, 0, 2)
    sources = jnp.arange(N_DOM, dtype=jnp.int32)[:, None]

    def aggregate_one(inputs):
        part_index, rows_in, source_slots, slot_counts, tile_block = inputs
        local_block = lax.dynamic_index_in_dim(partitions, part_index, 1, keepdims=False)
        border = partitions[:, sources, rows_in].reshape(D, N_DOM * SEND)
        extended = jnp.concatenate([local_block, border, hub_block], axis=1).reshape(D, EXT_TILES, TILE)
        picked = extended[:, source_slots]
        live_mask = (jnp.arange(SLOTS, dtype=jnp.int32)[None, :] < slot_counts[:, None]).astype(jnp.float32)
        picked = picked * live_mask[None, :, :, None]
        summed = jnp.einsum("ftkj,tkji->fti", picked, tile_block, precision=lax.Precision.HIGHEST)
        return summed.reshape(D, NODE_DEV)

    blocks = lax.map(aggregate_one, (jnp.arange(N_DOM, dtype=jnp.int32), incoming,
                                     tile_src.reshape(N_DOM, NODE_TILES, SLOTS),
                                     tile_count.reshape(N_DOM, NODE_TILES),
                                     tile_vals.reshape(N_DOM, NODE_TILES, SLOTS, TILE, TILE)))
    aggregated = blocks.transpose(1, 0, 2).reshape(D, NODES)
    output = jnp.tanh(jnp.dot(weight.T, aggregated, precision=lax.Precision.HIGHEST))
    pre_grad = cotangent * (1.0 - output * output)
    grad_weight = jnp.dot(aggregated, pre_grad.T, precision=lax.Precision.HIGHEST)
    return output, grad_weight
```

```python
import jax
import jax.numpy as jnp
from jax import lax
from jax.experimental import pallas as pl
from jax.experimental.pallas import tpu as pltpu
from jax.sharding import PartitionSpec as P

N_X, N_Z, N_Y = 4, 12, 8
N_DOM = N_X * N_Z
N_FEAT = 2 * N_Y
D = 256
TILE = 128
SHARE = D // N_FEAT
SLOTS = 6
OWN = 16
BORDER = 12
HUB_TILES = 6
HUBS = HUB_TILES * TILE
EXT = OWN + BORDER + HUB_TILES
LIVE_FIRST = 3
F32, BF16, I32 = jnp.float32, jnp.bfloat16, jnp.int32


def split(value):
    high = value.astype(BF16)
    return high, (value - high.astype(F32)).astype(BF16)


def dot3(a, b, dims):
    a_high, a_low = split(a)
    b_high, b_low = split(b)

    def one(u, v):
        return lax.dot_general(u, v, (dims, ((), ())), preferred_element_type=F32)

    return one(a_high, b_high) + (one(a_high, b_low) + one(a_low, b_high))


def pick(table, index):
    return jnp.take_along_axis(table, index, axis=1, mode="promise_in_bounds")


def loop(first, last, body):
    def step(i, carry):
        body(i)
        return carry

    lax.fori_loop(first, last, step, 0)


def kernel(
    features, tile_src, tile_count, send_rows, hub_owner, hub_row, weight, tile_vals, cotangent,
    output, grad_weight,
    vals, cot, source, stage, picked, ints, ints_smem,
    border_out, border_in, hub_out, hub_z, hub_x, weight_t,
    core_out, core_in, y_out, y_in, x_out, x_in, z_out, z_in, last_in,
    local_sems, send_sems, recv_sems,
):
    dom, feat = lax.axis_index("dom"), lax.axis_index("feat")
    z, x = dom // N_X, dom % N_X
    y, core = feat // 2, feat % 2

    def dom_peer(j):
        return lax.rem(dom + j, N_DOM)

    def feat_peer(j):
        return lax.rem(feat + j, N_FEAT)

    def remote(src, dst, which, device):
        return pltpu.make_async_remote_copy(
            src_ref=src, dst_ref=dst, send_sem=send_sems.at[which], recv_sem=recv_sems.at[which],
            device_id=device, device_id_type=pl.DeviceIdType.MESH,
        )

    def wait_all(ref, sem):
        pltpu.make_async_copy(ref, ref, sem).wait()

    barrier = pltpu.get_barrier_semaphore()
    loop(1, N_DOM, lambda j: pl.semaphore_signal(
        barrier, inc=1, device_id={"dom": dom_peer(j)}, device_id_type=pl.DeviceIdType.MESH))
    loop(1, N_FEAT, lambda j: pl.semaphore_signal(
        barrier, inc=1, device_id={"feat": feat_peer(j)}, device_id_type=pl.DeviceIdType.MESH))

    vals_copy = pltpu.make_async_copy(tile_vals, vals, local_sems.at[0])
    cot_copy = pltpu.make_async_copy(cotangent, cot, local_sems.at[1])
    vals_copy.start()
    cot_copy.start()

    lane8 = lax.broadcasted_iota(I32, (8, TILE), 1)
    row8 = lax.broadcasted_iota(I32, (8, TILE), 0)

    for t in range(OWN):
        source[t] = features[:, t * TILE : (t + 1) * TILE]
    lane1 = lax.broadcasted_iota(I32, (1, TILE), 1)
    listed = jnp.zeros((1, TILE), I32)
    for k in range(SLOTS):
        listed = jnp.where(lane1 == k, tile_src[0, k], listed)
    ints[pl.ds(feat, 1)] = listed[None]
    weight_t[pl.ds(feat, 1)] = jnp.transpose(weight[...])[None]

    owner = hub_owner[...]
    earlier = (lax.broadcasted_iota(I32, (HUBS, HUBS), 0) < lax.broadcasted_iota(I32, (HUBS, HUBS), 1))
    owned = (lax.broadcasted_iota(I32, (N_DOM, HUBS), 0) == owner).astype(F32)
    before = jnp.dot(owned.astype(BF16), earlier.astype(F32).astype(BF16), preferred_element_type=F32)
    rank = jnp.dot(jnp.ones((8, N_DOM), BF16), (owned * before).astype(BF16), preferred_element_type=F32)
    rank = rank.astype(I32)
    mine = owner == dom
    place = lax.broadcasted_iota(I32, (TILE, HUBS), 0) % 64
    chosen = (mine & (rank[0:1] == place)).astype(F32).astype(BF16)
    row = hub_row[...]
    row_parts = jnp.concatenate([jnp.broadcast_to(row // 16, (8, HUBS)), jnp.broadcast_to(row % 16, (8, HUBS))], axis=0)
    my_rows = lax.dot_general(
        row_parts.astype(F32).astype(BF16), chosen, (((1,), (1,)), ((), ())), preferred_element_type=F32
    )
    my_rows = my_rows[0:8].astype(I32) * 16 + my_rows[8:16].astype(I32)

    def columns(v, index):
        low, high = index % TILE, index // TILE
        found = jnp.zeros((8, TILE), F32)
        for t in range(OWN):
            part = pick(features[8 * v : 8 * v + 8, t * TILE : (t + 1) * TILE], low)
            found = jnp.where(high == t, part, found)
        return found

    hub_out[...] = jnp.where(lane8 < 64, columns(0, my_rows), columns(1, my_rows))

    group4 = lax.broadcasted_iota(I32, (4, TILE), 1) // 32
    in_group = [group4 == (t + x) % 4 for t in range(4)]

    def border_tile(q):
        rows = jnp.broadcast_to(send_rows[pl.ds(q, 1), :], (8, TILE))
        quarter = []
        for v in range(2):
            turned = pick(rows, (lane8 - 32 * (2 * v + row8 // 4 + x)) % TILE)
            found = columns(v, turned)
            quarter += [found[0:4], found[4:8]]
        for d in range(4):
            message = quarter[0]
            for a in range(4):
                message = jnp.where(in_group[(a + d) % 4], quarter[a], message)
            border_out[pl.ds(4 * q + d, 1)] = message[None]

    loop(0, BORDER, border_tile)

    pl.semaphore_wait(barrier, N_DOM - 1 + N_FEAT - 1)

    def z_device(z_to):
        return {"dom": z_to * N_X + x}

    def x_device(x_to):
        return {"dom": z * N_X + x_to}

    def y_device(y_to):
        return {"feat": y_to * 2 + core}

    loop(1, N_Z, lambda j: remote(hub_out, hub_z.at[z], 0, z_device(lax.rem(z + j, N_Z))).start())
    loop(1, N_DOM, lambda j: remote(
        border_out.at[dom_peer(j)], border_in.at[dom], 1, {"dom": dom_peer(j)}).start())
    loop(1, N_FEAT, lambda j: remote(ints.at[feat], ints.at[feat], 2, {"feat": feat_peer(j)}).start())
    loop(1, N_FEAT, lambda j: remote(
        source.at[feat_peer(j)], picked.at[0, feat], 3, {"feat": feat_peer(j)}).start())
    loop(1, N_FEAT, lambda j: remote(weight_t.at[feat], weight_t.at[feat], 4, {"feat": feat_peer(j)}).start())

    picked[0, pl.ds(feat, 1)] = source[pl.ds(feat, 1)]
    border_in[pl.ds(dom, 1)] = border_out[pl.ds(dom, 1)]
    hub_z[pl.ds(z, 1)] = hub_out[...][None]

    wait_all(hub_z.at[pl.ds(0, N_Z - 1)], recv_sems.at[0])
    loop(1, N_X, lambda j: remote(hub_z, hub_x.at[x], 5, x_device(lax.rem(x + j, N_X))).start())
    hub_x[pl.ds(x, 1)] = hub_z[...][None]

    wait_all(ints.at[pl.ds(0, N_FEAT - 1)], recv_sems.at[2])
    ints_copy = pltpu.make_async_copy(ints, ints_smem, local_sems.at[2])
    ints_copy.start()

    wait_all(border_in.at[pl.ds(0, N_DOM - 1)], recv_sems.at[1])
    quarter_of = [2 * v + row8 // 4 for v in range(2)]

    def border_arrived(q):
        pieces = []
        for e in range(4):
            piece = border_in[pl.ds(4 * q + e, 1)][0]
            pieces.append(jnp.concatenate([piece, piece], axis=0))
        for v in range(2):
            mixed = pieces[0]
            for e in range(1, 4):
                mixed = jnp.where(lane8 // 32 == (quarter_of[v] + e + x) % 4, pieces[e], mixed)
            source[pl.ds(OWN + q, 1), 8 * v : 8 * v + 8] = pick(mixed, (lane8 + 32 * (quarter_of[v] + x)) % TILE)[None]

    loop(0, BORDER, border_arrived)

    wait_all(hub_x.at[pl.ds(0, N_X - 1)], recv_sems.at[5])
    owner8 = jnp.broadcast_to(owner, (8, HUBS))
    at = (owner8 % 2) * 64 + rank
    pair = owner8 // 2

    def hub_pair(p, found):
        even = hub_x[2 * (p % 2), p // 2]
        odd = hub_x[2 * (p % 2) + 1, p // 2]
        tables = (
            jnp.where(lane8 < 64, even, pltpu.roll(odd, 64, 1)),
            jnp.where(lane8 < 64, pltpu.roll(even, 64, 1), odd),
        )
        result = []
        for q in range(HUB_TILES):
            cut = slice(q * TILE, (q + 1) * TILE)
            for v in range(2):
                result.append(jnp.where(pair[:, cut] == p, pick(tables[v], at[:, cut]), found[2 * q + v]))
        return tuple(result)

    found = lax.fori_loop(0, N_DOM // 2, hub_pair, (jnp.zeros((8, TILE), F32),) * (2 * HUB_TILES))
    for q in range(HUB_TILES):
        for v in range(2):
            source[OWN + BORDER + q, 8 * v : 8 * v + 8] = found[2 * q + v]

    ints_copy.wait()

    def send_slots(first, last, which):
        def to_peer(j):
            peer = feat_peer(j)
            for k in range(first, last):
                stage[peer, k] = source[ints_smem[peer, 0, k]]
            cut = pl.ds(first, last - first)
            remote(stage.at[peer, cut], picked.at[cut, feat], which, {"feat": peer}).start()

        loop(1, N_FEAT, to_peer)
        for k in range(first, last):
            picked[k, feat] = source[tile_src[0, k]]

    send_slots(1, LIVE_FIRST, 6)
    send_slots(LIVE_FIRST, SLOTS, 7)

    vals_copy.wait()
    count = tile_count[0]

    def aggregate(k):
        live = jnp.where(k < count, 1.0, 0.0).astype(F32)
        return dot3(picked[k].reshape(D, TILE), vals[0, k] * live, ((1,), (0,)))

    def arrived(first, last, which):
        wait_all(picked.at[pl.ds(first, last - first), pl.ds(0, N_FEAT - 1)], recv_sems.at[which])

    arrived(0, 1, 3)
    aggregated = aggregate(0)
    arrived(1, LIVE_FIRST, 6)
    for k in range(1, LIVE_FIRST):
        aggregated += aggregate(k)
    wait_all(weight_t.at[pl.ds(0, N_FEAT - 1)], recv_sems.at[4])
    cot_copy.wait()
    arrived(LIVE_FIRST, SLOTS, 7)
    for k in range(LIVE_FIRST, SLOTS):
        aggregated += aggregate(k)

    result = jnp.tanh(dot3(weight_t[...].reshape(D, D), aggregated, ((1,), (0,))))
    output[...] = result
    pre_grad = cot[...] * (1.0 - result * result)
    partial = dot3(pre_grad, aggregated, ((1,), (1,)))

    for c in range(2):
        for w in range(N_Y):
            first = SHARE * (2 * w + c)
            core_out[c, w] = partial[first : first + SHARE]
    other = 1 - core
    to_core = remote(core_out.at[other], core_in, 8, {"feat": y * 2 + other})
    to_core.start()
    to_core.wait_recv()
    y_out[...] = core_out[core] + core_in[...]
    loop(1, N_Y, lambda j: remote(
        y_out.at[lax.rem(y + j, N_Y)], y_in.at[y], 9, y_device(lax.rem(y + j, N_Y))).start())
    y_in[pl.ds(y, 1)] = y_out[pl.ds(y, 1)]
    wait_all(y_in.at[pl.ds(0, N_Y - 1)], recv_sems.at[9])
    total = y_in[0]
    for w in range(1, N_Y):
        total += y_in[w]
    for j in range(N_X):
        x_out[j] = total[8 * (j // 2) : 8 * (j // 2) + 8, TILE * (j % 2) : TILE * (j % 2) + TILE]
    loop(1, N_X, lambda j: remote(
        x_out.at[lax.rem(x + j, N_X)], x_in.at[x], 10, x_device(lax.rem(x + j, N_X))).start())
    x_in[pl.ds(x, 1)] = x_out[pl.ds(x, 1)]
    wait_all(x_in.at[pl.ds(0, N_X - 1)], recv_sems.at[10])
    z_out[...] = (x_in[0] + x_in[1]) + (x_in[2] + x_in[3])
    loop(1, N_Z, lambda j: remote(z_out, z_in.at[z], 11, z_device(lax.rem(z + j, N_Z))).start())
    z_in[pl.ds(z, 1)] = z_out[...][None]
    wait_all(z_in.at[pl.ds(0, N_Z - 1)], recv_sems.at[11])
    chunk = z_in[0]
    for w in range(1, N_Z):
        chunk += z_in[w]
    last_in[pl.ds(x, 1)] = chunk[None]
    loop(1, N_X, lambda j: remote(last_in.at[x], last_in.at[x], 12, x_device(lax.rem(x + j, N_X))).start())
    wait_all(last_in.at[pl.ds(0, N_X - 1)], recv_sems.at[12])
    whole = jnp.concatenate(
        [jnp.concatenate([last_in[0], last_in[1]], axis=1), jnp.concatenate([last_in[2], last_in[3]], axis=1)], axis=0
    )
    grad_weight[...] = jnp.transpose(whole)

    wait_all(hub_z.at[pl.ds(0, N_Z - 1)], send_sems.at[0])
    wait_all(border_in.at[pl.ds(0, N_DOM - 1)], send_sems.at[1])
    wait_all(ints.at[pl.ds(0, N_FEAT - 1)], send_sems.at[2])
    wait_all(picked.at[0, pl.ds(0, N_FEAT - 1)], send_sems.at[3])
    wait_all(weight_t.at[pl.ds(0, N_FEAT - 1)], send_sems.at[4])
    wait_all(hub_x.at[pl.ds(0, N_X - 1)], send_sems.at[5])
    wait_all(picked.at[pl.ds(1, LIVE_FIRST - 1), pl.ds(0, N_FEAT - 1)], send_sems.at[6])
    wait_all(picked.at[pl.ds(LIVE_FIRST, SLOTS - LIVE_FIRST), pl.ds(0, N_FEAT - 1)], send_sems.at[7])
    to_core.wait_send()
    wait_all(y_in.at[pl.ds(0, N_Y - 1)], send_sems.at[9])
    wait_all(x_in.at[pl.ds(0, N_X - 1)], send_sems.at[10])
    wait_all(z_in.at[pl.ds(0, N_Z - 1)], send_sems.at[11])
    wait_all(last_in.at[pl.ds(0, N_X - 1)], send_sems.at[12])


def on_device(
    features, tile_vals, tile_src, tile_count, send_rows, hub_owner, hub_row, weight, cotangent
):
    vmem, smem = pl.BlockSpec(memory_space=pltpu.VMEM), pl.BlockSpec(memory_space=pltpu.SMEM)
    anywhere = pl.BlockSpec(memory_space=pl.ANY)
    scratch = [
        pltpu.VMEM(tile_vals.shape, F32),
        pltpu.VMEM(cotangent.shape, F32),
        pltpu.VMEM((EXT, SHARE, TILE), F32),
        pltpu.VMEM((N_FEAT, SLOTS, SHARE, TILE), F32),
        pltpu.VMEM((SLOTS, N_FEAT, SHARE, TILE), F32),
        pltpu.VMEM((N_FEAT, 1, TILE), I32),
        pltpu.SMEM((N_FEAT, 1, TILE), I32),
        pltpu.VMEM((N_DOM, 4, TILE), F32),
        pltpu.VMEM((N_DOM, 4, TILE), F32),
        pltpu.VMEM((8, TILE), F32),
        pltpu.VMEM((N_Z, 8, TILE), F32),
        pltpu.VMEM((N_X, N_Z, 8, TILE), F32),
        pltpu.VMEM((N_FEAT, SHARE, D), F32),
        pltpu.VMEM((2, N_Y, SHARE, D), F32),
        pltpu.VMEM((N_Y, SHARE, D), F32),
        pltpu.VMEM((N_Y, SHARE, D), F32),
        pltpu.VMEM((N_Y, SHARE, D), F32),
        pltpu.VMEM((N_X, 8, TILE), F32),
        pltpu.VMEM((N_X, 8, TILE), F32),
        pltpu.VMEM((8, TILE), F32),
        pltpu.VMEM((N_Z, 8, TILE), F32),
        pltpu.VMEM((N_X, 8, TILE), F32),
        pltpu.SemaphoreType.DMA((3,)),
        pltpu.SemaphoreType.DMA((13,)),
        pltpu.SemaphoreType.DMA((13,)),
    ]
    return pl.pallas_call(
        kernel,
        out_shape=(
            jax.ShapeDtypeStruct(cotangent.shape, F32),
            jax.ShapeDtypeStruct(weight.shape, F32),
        ),
        in_specs=[vmem, smem, smem, vmem, vmem, vmem, vmem, anywhere, anywhere],
        out_specs=(vmem, vmem),
        scratch_shapes=scratch,
        compiler_params=pltpu.CompilerParams(
            collective_id=0, has_side_effects=True, vmem_limit_bytes=40 * 1024 * 1024
        ),
    )(
        features, tile_src, tile_count, send_rows.reshape(BORDER, TILE),
        hub_owner.reshape(1, HUBS), hub_row.reshape(1, HUBS), weight, tile_vals, cotangent,
    )


def solution(mesh):
    in_specs = (
        P("feat", "dom"),
        P(("dom", "feat"), None, None, None),
        P(("dom", "feat"), None),
        P(("dom", "feat")),
        P("dom", None),
        P(),
        P(),
        P(None, "feat"),
        P(None, ("dom", "feat")),
    )
    out_specs = (P(None, ("dom", "feat")), P(None, "feat"))
    return jax.shard_map(
        on_device, mesh=mesh, in_specs=in_specs, out_specs=out_specs, check_vma=False
    )
```

```python
import jax
import jax.numpy as jnp
from jax import lax
from jax.experimental import pallas as pl
from jax.experimental.pallas import tpu as pltpu
from jax.sharding import PartitionSpec as P

N_X, N_Z, N_Y = 4, 12, 8
N_DOM = N_X * N_Z
N_FEAT = 2 * N_Y
D = 256
TILE = 128
SHARE = D // N_FEAT
SEND = 32
SLOTS = 6
OWN = 16
BORDER = 12
HUB_TILES = 6
HUBS = HUB_TILES * TILE
EXT = OWN + BORDER + HUB_TILES
F32, BF16, I32 = jnp.float32, jnp.bfloat16, jnp.int32


def split(value):
    high = value.astype(BF16)
    return high, (value - high.astype(F32)).astype(BF16)


def dot3(a, b, dims):
    a_high, a_low = split(a)
    b_high, b_low = split(b)

    def one(u, v):
        return lax.dot_general(u, v, (dims, ((), ())), preferred_element_type=F32)

    return one(a_high, b_high) + (one(a_high, b_low) + one(a_low, b_high))


def pick(table, index):
    return jnp.take_along_axis(table, index, axis=1, mode="promise_in_bounds")


def loop(first, last, body):
    def step(i, carry):
        body(i)
        return carry

    lax.fori_loop(first, last, step, 0)


def far_first(i, n):
    return n // 2 + (i % 2) * ((i + 1) // 2) - (1 - i % 2) * (i // 2)


def each_dom(body):
    def of_z(i):
        for dx in (2, 1, 3, 0):
            body(i, dx)

    loop(0, N_Z - 1, of_z)
    for dx in (2, 1, 3):
        body(N_Z - 1, dx)


def kernel(
    tile_src, tile_count_hbm, features_hbm, send_rows_hbm, hub_owner_hbm, hub_row_hbm, weight_hbm, tile_vals, cotangent,
    output_hbm, grad_hbm,
    output, grad_weight, tile_count, features, send_rows, hub_owner, hub_row, row_list, vals, cot, source, stage, picked, ints, ints_smem,
    border_out, border_in, hub_out, hub_z, hub_part, hub_x, weight_t,
    core_out, core_in, y_out, y_in, sized, z_out, z_in, last_in,
    local_sems, send_sems, recv_sems,
):
    dom, feat = lax.axis_index("dom"), lax.axis_index("feat")
    z, x = dom // N_X, dom % N_X
    y, core = feat // 2, feat % 2

    def dom_far(i, dx):
        return lax.rem(z + far_first(i, N_Z), N_Z) * N_X + lax.rem(x + dx, N_X)

    def feat_far(i):
        t = N_FEAT - 2 - i
        j = (1 - t % 2) * (t // 2 + 1) + (t % 2) * (N_FEAT - 1 - t // 2)
        return lax.rem(feat + j, N_FEAT)

    def remote(src, dst, which, device):
        return pltpu.make_async_remote_copy(
            src_ref=src, dst_ref=dst, send_sem=send_sems.at[which], recv_sem=recv_sems.at[which],
            device_id=device, device_id_type=pl.DeviceIdType.MESH,
        )

    def wait_all(ref, sem):
        pltpu.make_async_copy(ref, ref, sem).wait()

    def wait_most(ref, sem):
        flat = sized.at[pl.ds(0, N_Y * N_X - 1)]
        wait_all(flat, sem)

    def fetch(src, dst, which):
        copy = pltpu.make_async_copy(src, dst, local_sems.at[which])
        copy.start()
        return copy

    barrier = pltpu.get_barrier_semaphore()
    each_dom(lambda i, dx: pl.semaphore_signal(
        barrier, inc=1, device_id={"dom": dom_far(i, dx)}, device_id_type=pl.DeviceIdType.MESH))
    loop(0, N_FEAT - 1, lambda i: pl.semaphore_signal(
        barrier, inc=1, device_id={"feat": feat_far(i)}, device_id_type=pl.DeviceIdType.MESH))

    owner_copy = fetch(hub_owner_hbm, hub_owner, 5)
    hub_row_copy = fetch(hub_row_hbm, hub_row, 6)
    features_copy = fetch(features_hbm, features, 3)
    rows_copy = fetch(send_rows_hbm, send_rows, 4)
    weight_copy = fetch(weight_hbm, weight_t.at[y, core], 7)
    count_copy = fetch(tile_count_hbm, tile_count, 8)
    vals_copy = fetch(tile_vals, vals, 0)
    cot_copy = fetch(cotangent, cot, 1)

    lane8 = lax.broadcasted_iota(I32, (8, TILE), 1)
    row8 = lax.broadcasted_iota(I32, (8, TILE), 0)

    features_copy.wait()
    for t in range(OWN):
        source[t] = features[:, t * TILE : (t + 1) * TILE]
    lane1 = lax.broadcasted_iota(I32, (1, TILE), 1)
    listed = jnp.zeros((1, TILE), I32)
    for k in range(SLOTS):
        listed = jnp.where(lane1 == k, tile_src[0, k], listed)
    ints[pl.ds(feat, 1)] = listed[None]

    owner_copy.wait()
    hub_row_copy.wait()
    owner = hub_owner[...].reshape(1, HUBS)
    earlier = (lax.broadcasted_iota(I32, (HUBS, HUBS), 0) < lax.broadcasted_iota(I32, (HUBS, HUBS), 1))
    owned = (lax.broadcasted_iota(I32, (N_DOM, HUBS), 0) == owner).astype(F32)
    before = jnp.dot(owned.astype(BF16), earlier.astype(F32).astype(BF16), preferred_element_type=F32)
    rank = jnp.dot(jnp.ones((8, N_DOM), BF16), (owned * before).astype(BF16), preferred_element_type=F32)
    rank = rank.astype(I32)
    mine = owner == dom
    place = lax.broadcasted_iota(I32, (TILE, HUBS), 0) % 64
    chosen = (mine & (rank[0:1] == place)).astype(F32).astype(BF16)
    row = hub_row[...].reshape(1, HUBS)
    row_parts = jnp.concatenate([jnp.broadcast_to(row // 16, (8, HUBS)), jnp.broadcast_to(row % 16, (8, HUBS))], axis=0)
    my_rows = lax.dot_general(
        row_parts.astype(F32).astype(BF16), chosen, (((1,), (1,)), ((), ())), preferred_element_type=F32
    )
    my_rows = my_rows[0:8].astype(I32) * 16 + my_rows[8:16].astype(I32)

    def columns(v, index):
        low, high = index % TILE, index // TILE
        found = jnp.zeros((8, TILE), F32)
        for t in range(OWN):
            part = pick(features[8 * v : 8 * v + 8, t * TILE : (t + 1) * TILE], low)
            found = jnp.where(high == t, part, found)
        return found

    hub_out[...] = jnp.where(lane8 < 64, columns(0, my_rows), columns(1, my_rows))

    rows_copy.wait()
    repeat = lax.broadcasted_iota(I32, (SEND, TILE), 1) % SEND == lax.broadcasted_iota(I32, (SEND, TILE), 0)
    row_list[...] = lax.dot_general(
        send_rows[...].astype(F32), repeat.astype(F32), (((0,), (0,)), ((), ())),
        precision=lax.Precision.HIGHEST, preferred_element_type=F32,
    ).astype(I32)

    group4 = lax.broadcasted_iota(I32, (4, TILE), 1) // 32
    in_group = [group4 == (t + x) % 4 for t in range(4)]

    def border_tile(q):
        lists = [jnp.broadcast_to(row_list[pl.ds(4 * q + d, 1), :], (8, TILE)) for d in range(4)]
        quarter = []
        for v in range(2):
            turned = lists[0]
            for d in range(1, 4):
                turned = jnp.where(lane8 // 32 == (d + 2 * v + row8 // 4 + x) % 4, lists[d], turned)
            found = columns(v, turned)
            quarter += [found[0:4], found[4:8]]
        for d in range(4):
            message = quarter[0]
            for a in range(4):
                message = jnp.where(in_group[(a + d) % 4], quarter[a], message)
            border_out[pl.ds(4 * q + d, 1)] = message[None]

    loop(0, BORDER, border_tile)

    weight_copy.wait()
    pl.semaphore_wait(barrier, N_DOM - 1 + N_FEAT - 1)

    def z_device(z_to):
        return {"dom": z_to * N_X + x}

    def x_device(x_to):
        return {"dom": z * N_X + x_to}

    def y_device(y_to):
        return {"feat": y_to * 2 + core}

    loop(0, N_Z - 1, lambda i: remote(
        hub_out, hub_z.at[z], 0, z_device(lax.rem(z + far_first(i, N_Z), N_Z))).start())
    each_dom(lambda i, dx: remote(
        border_out.at[dom_far(i, dx)], border_in.at[dom], 1, {"dom": dom_far(i, dx)}).start())
    loop(0, N_FEAT - 1, lambda i: remote(ints.at[feat], ints.at[feat], 2, {"feat": feat_far(i)}).start())
    loop(0, N_FEAT - 1, lambda i: remote(
        source.at[feat_far(i)], picked.at[0, feat], 3, {"feat": feat_far(i)}).start())
    loop(0, N_Y - 1, lambda i: remote(
        weight_t.at[y, core], weight_t.at[y, core], 4, y_device(lax.rem(y + far_first(i, N_Y), N_Y))).start())

    picked[0, pl.ds(feat, 1)] = source[pl.ds(feat, 1)]
    border_in[pl.ds(dom, 1)] = border_out[pl.ds(dom, 1)]
    hub_z[pl.ds(z, 1)] = hub_out[...][None]

    wait_all(hub_z.at[pl.ds(0, N_Z - 1)], recv_sems.at[0])
    owner8 = jnp.broadcast_to(owner, (8, HUBS))
    at = (owner8 // N_X % 2) * 64 + rank
    pair = jnp.where(owner8 % N_X == x, owner8 // (2 * N_X), N_Z)
    found = [jnp.zeros((8, TILE), F32)] * (2 * HUB_TILES)
    for p in range(N_Z // 2):
        even, odd = hub_z[2 * p], hub_z[2 * p + 1]
        tables = (
            jnp.where(lane8 < 64, even, pltpu.roll(odd, 64, 1)),
            jnp.where(lane8 < 64, pltpu.roll(even, 64, 1), odd),
        )
        for q in range(HUB_TILES):
            span = slice(q * TILE, (q + 1) * TILE)
            for v in range(2):
                found[2 * q + v] = jnp.where(pair[:, span] == p, pick(tables[v], at[:, span]), found[2 * q + v])
    for q in range(HUB_TILES):
        for v in range(2):
            hub_part[q, 8 * v : 8 * v + 8] = found[2 * q + v]
    loop(1, N_X, lambda j: remote(hub_part, hub_x.at[x], 5, x_device(lax.rem(x + j, N_X))).start())
    hub_x[pl.ds(x, 1)] = hub_part[...][None]

    wait_all(ints.at[pl.ds(0, N_FEAT - 1)], recv_sems.at[2])
    ints_copy = pltpu.make_async_copy(ints, ints_smem, local_sems.at[2])
    ints_copy.start()

    wait_all(border_in.at[pl.ds(0, N_DOM - 1)], recv_sems.at[1])
    quarter_of = [2 * v + row8 // 4 for v in range(2)]

    def border_arrived(q):
        pieces = []
        for e in range(4):
            piece = border_in[pl.ds(4 * q + e, 1)][0]
            pieces.append(jnp.concatenate([piece, piece], axis=0))
        for v in range(2):
            mixed = pieces[0]
            for e in range(1, 4):
                mixed = jnp.where(lane8 // 32 == (quarter_of[v] + e + x) % 4, pieces[e], mixed)
            source[pl.ds(OWN + q, 1), 8 * v : 8 * v + 8] = pick(mixed, (lane8 + 32 * (quarter_of[v] + x)) % TILE)[None]

    loop(0, BORDER, border_arrived)

    ints_copy.wait()

    def send_slots(first, last, which):
        def to_peer(i):
            peer = feat_far(i)
            for k in range(first, last):
                stage[peer, k] = source[ints_smem[peer, 0, k]]
            some = pl.ds(first, last - first)
            remote(stage.at[peer, some], picked.at[some, feat], which, {"feat": peer}).start()

        loop(0, N_FEAT - 1, to_peer)
        for k in range(first, last):
            picked[k, feat] = source[tile_src[0, k]]

    send_slots(1, 2, 6)
    wait_all(hub_x.at[pl.ds(0, N_X - 1)], recv_sems.at[5])
    for q in range(HUB_TILES):
        source[OWN + BORDER + q] = (hub_x[0, q] + hub_x[1, q]) + (hub_x[2, q] + hub_x[3, q])
    send_slots(2, 4, 7)
    send_slots(4, SLOTS, 10)
    wait_all(weight_t.at[pl.ds(0, N_Y - 1), 0], recv_sems.at[4])
    other = 1 - core
    weight_on = remote(weight_t.at[:, core], weight_t.at[:, core], 12, {"feat": y * 2 + other})
    weight_on.start()

    vals_copy.wait()
    count_copy.wait()
    count = tile_count[0]

    def aggregate(k):
        live = jnp.where(k < count, 1.0, 0.0).astype(F32)
        return dot3(picked[k].reshape(D, TILE), vals[0, k] * live, ((1,), (0,)))

    def arrived(first, last, which):
        wait_all(picked.at[pl.ds(first, last - first), pl.ds(0, N_FEAT - 1)], recv_sems.at[which])

    arrived(0, 1, 3)
    aggregated = aggregate(0)
    for first, last, which in ((1, 2, 6), (2, 4, 7), (4, SLOTS, 10)):
        if last == SLOTS:
            weight_on.wait_recv()
            cot_copy.wait()
        arrived(first, last, which)
        for k in range(first, last):
            aggregated += aggregate(k)

    result = jnp.tanh(dot3(weight_t[...].reshape(D, D), aggregated, ((1,), (0,))))
    output[...] = result
    output_copy = fetch(output, output_hbm, 9)
    pre_grad = cot[...] * (1.0 - result * result)
    partial = dot3(pre_grad, aggregated, ((1,), (1,)))

    for c in range(2):
        for w in range(N_Y):
            for j in range(N_X):
                top, left = SHARE * (2 * w + c) + 8 * (j // 2), TILE * (j % 2)
                core_out[c, w, j] = partial[top : top + 8, left : left + TILE]
    to_core = remote(core_out.at[other], core_in, 8, {"feat": y * 2 + other})
    to_core.start()
    to_core.wait_recv()
    y_out[...] = core_out[core] + core_in[...]

    def to_column(i, dx):
        y_to, x_to = lax.rem(y + far_first(i, N_Y), N_Y), lax.rem(x + dx, N_X)
        device = {"dom": z * N_X + x_to, "feat": y_to * 2 + core}
        remote(y_out.at[y_to, x_to], y_in.at[y, x], 9, device).start()

    def of_y(i):
        for dx in (2, 1, 3, 0):
            to_column(i, dx)

    loop(0, N_Y - 1, of_y)
    for dx in (2, 1, 3):
        to_column(N_Y - 1, dx)
    y_in[pl.ds(y, 1), pl.ds(x, 1)] = y_out[pl.ds(y, 1), pl.ds(x, 1)]
    wait_most(y_in, recv_sems.at[9])
    total = [y_in[w, 0] + y_in[w, 1] + (y_in[w, 2] + y_in[w, 3]) for w in range(N_Y)]
    while len(total) > 1:
        total = [a + b for a, b in zip(total[0::2], total[1::2])]
    z_out[...] = total[0]
    loop(0, N_Z - 1, lambda i: remote(
        z_out, z_in.at[z], 11, z_device(lax.rem(z + far_first(i, N_Z), N_Z))).start())
    z_in[pl.ds(z, 1)] = z_out[...][None]
    wait_all(z_in.at[pl.ds(0, N_Z - 1)], recv_sems.at[11])
    thirds = [z_in[w] + z_in[w + 1] + (z_in[w + 2] + z_in[w + 3]) for w in range(0, N_Z, 4)]
    chunk = thirds[0] + thirds[1] + thirds[2]
    last_in[pl.ds(x, 1)] = chunk[None]
    loop(1, N_X, lambda j: remote(last_in.at[x], last_in.at[x], 13, x_device(lax.rem(x + j, N_X))).start())
    wait_all(last_in.at[pl.ds(0, N_X - 1)], recv_sems.at[13])
    whole = jnp.concatenate(
        [jnp.concatenate([last_in[0], last_in[1]], axis=1), jnp.concatenate([last_in[2], last_in[3]], axis=1)], axis=0
    )
    grad_weight[...] = whole
    fetch(grad_weight, grad_hbm, 10).wait()
    output_copy.wait()

    wait_all(hub_z.at[pl.ds(0, N_Z - 1)], send_sems.at[0])
    wait_all(border_in.at[pl.ds(0, N_DOM - 1)], send_sems.at[1])
    wait_all(ints.at[pl.ds(0, N_FEAT - 1)], send_sems.at[2])
    wait_all(picked.at[0, pl.ds(0, N_FEAT - 1)], send_sems.at[3])
    wait_all(weight_t.at[pl.ds(0, N_Y - 1), 0], send_sems.at[4])
    wait_all(hub_x.at[pl.ds(0, N_X - 1)], send_sems.at[5])
    for first, last, which in ((1, 2, 6), (2, 4, 7), (4, SLOTS, 10)):
        wait_all(picked.at[pl.ds(first, last - first), pl.ds(0, N_FEAT - 1)], send_sems.at[which])
    weight_on.wait_send()
    to_core.wait_send()
    wait_most(y_in, send_sems.at[9])
    wait_all(z_in.at[pl.ds(0, N_Z - 1)], send_sems.at[11])
    wait_all(last_in.at[pl.ds(0, N_X - 1)], send_sems.at[13])


def hand_on(output, grad_weight, output_to, grad_to, sems):
    copies = (
        pltpu.make_async_copy(output, output_to, sems.at[0]),
        pltpu.make_async_copy(grad_weight, grad_to, sems.at[1]),
    )
    for copy in copies:
        copy.start()
    for copy in copies:
        copy.wait()


def on_device(
    features, tile_vals, tile_src, tile_count, send_rows, hub_owner, hub_row, weight, cotangent
):
    smem = pl.BlockSpec(memory_space=pltpu.SMEM)
    hbm = pl.BlockSpec(memory_space=pltpu.HBM)
    scratch = [
        pltpu.VMEM(cotangent.shape, F32),
        pltpu.VMEM((SHARE, D), F32),
        pltpu.SMEM(tile_count.shape, I32),
        pltpu.VMEM(features.shape, F32),
        pltpu.VMEM((SEND, N_DOM), I32),
        pltpu.VMEM((HUBS,), I32),
        pltpu.VMEM((HUBS,), I32),
        pltpu.VMEM((N_DOM, TILE), I32),
        pltpu.VMEM(tile_vals.shape, F32),
        pltpu.VMEM(cotangent.shape, F32),
        pltpu.VMEM((EXT, SHARE, TILE), F32),
        pltpu.VMEM((N_FEAT, SLOTS, SHARE, TILE), F32),
        pltpu.VMEM((SLOTS, N_FEAT, SHARE, TILE), F32),
        pltpu.VMEM((N_FEAT, 1, TILE), I32),
        pltpu.SMEM((N_FEAT, 1, TILE), I32),
        pltpu.VMEM((N_DOM, 4, TILE), F32),
        pltpu.VMEM((N_DOM, 4, TILE), F32),
        pltpu.VMEM((8, TILE), F32),
        pltpu.VMEM((N_Z, 8, TILE), F32),
        pltpu.VMEM((HUB_TILES, SHARE, TILE), F32),
        pltpu.VMEM((N_X, HUB_TILES, SHARE, TILE), F32),
        pltpu.VMEM((N_Y, 2, SHARE, D), F32),
        pltpu.VMEM((2, N_Y, N_X, 8, TILE), F32),
        pltpu.VMEM((N_Y, N_X, 8, TILE), F32),
        pltpu.VMEM((N_Y, N_X, 8, TILE), F32),
        pltpu.VMEM((N_Y, N_X, 8, TILE), F32),
        pltpu.VMEM((N_Y * N_X, 8, TILE), F32),
        pltpu.VMEM((8, TILE), F32),
        pltpu.VMEM((N_Z, 8, TILE), F32),
        pltpu.VMEM((N_X, 8, TILE), F32),
        pltpu.SemaphoreType.DMA((11,)),
        pltpu.SemaphoreType.DMA((14,)),
        pltpu.SemaphoreType.DMA((14,)),
    ]
    results = (
        jax.ShapeDtypeStruct(cotangent.shape, F32),
        jax.ShapeDtypeStruct((SHARE, D), F32),
    )
    made = pl.pallas_call(
        kernel,
        out_shape=results,
        in_specs=[smem] + [hbm] * 8,
        out_specs=(hbm, hbm),
        scratch_shapes=scratch,
        compiler_params=pltpu.CompilerParams(
            collective_id=0, has_side_effects=True, vmem_limit_bytes=60 * 1024 * 1024
        ),
    )(
        tile_src, tile_count, features, send_rows.T, hub_owner, hub_row, weight.T, tile_vals, cotangent
    )
    output, grad_weight = pl.pallas_call(
        hand_on,
        out_shape=results,
        in_specs=[hbm, hbm],
        out_specs=(hbm, hbm),
        scratch_shapes=[pltpu.SemaphoreType.DMA((2,))],
        compiler_params=pltpu.CompilerParams(vmem_limit_bytes=60 * 1024 * 1024),
    )(*made)
    return output, grad_weight.T


def solution(mesh):
    in_specs = (
        P("feat", "dom"),
        P(("dom", "feat"), None, None, None),
        P(("dom", "feat"), None),
        P(("dom", "feat")),
        P("dom", None),
        P(),
        P(),
        P(None, "feat"),
        P(None, ("dom", "feat")),
    )
    out_specs = (P(None, ("dom", "feat")), P(None, "feat"))
    return jax.shard_map(
        on_device, mesh=mesh, in_specs=in_specs, out_specs=out_specs, check_vma=False
    )
```

```python
import jax
import jax.numpy as jnp
from jax import lax
from jax.experimental import pallas as pl
from jax.experimental.pallas import tpu as pltpu
from jax.sharding import PartitionSpec as P

N_X, N_Z, N_Y = 4, 12, 8
N_DOM = N_X * N_Z
N_FEAT = 2 * N_Y
D = 256
TILE = 128
SHARE = D // N_FEAT
SEND = 32
SLOTS = 6
OWN = 16
BORDER = 12
HUB_TILES = 6
HUBS = HUB_TILES * TILE
EXT = OWN + BORDER + HUB_TILES
F32, BF16, I32 = jnp.float32, jnp.bfloat16, jnp.int32


def split(value):
    high = value.astype(BF16)
    return high, (value - high.astype(F32)).astype(BF16)


def dot3(a, b, dims):
    a_high, a_low = split(a)
    b_high, b_low = split(b)

    def one(u, v):
        return lax.dot_general(u, v, (dims, ((), ())), preferred_element_type=F32)

    return one(a_high, b_high) + (one(a_high, b_low) + one(a_low, b_high))


def pick(table, index):
    return jnp.take_along_axis(table, index, axis=1, mode="promise_in_bounds")


def loop(first, last, body):
    def step(i, carry):
        body(i)
        return carry

    lax.fori_loop(first, last, step, 0)


def far_first(i, n):
    return n // 2 + (i % 2) * ((i + 1) // 2) - (1 - i % 2) * (i // 2)


def each_dom(body):
    def of_z(i):
        for dx in (2, 1, 3, 0):
            body(i, dx)

    loop(0, N_Z - 1, of_z)
    for dx in (2, 1, 3):
        body(N_Z - 1, dx)


def kernel(
    tile_src, tile_count_hbm, features_hbm, send_rows_hbm, hub_owner_hbm, hub_row_hbm, weight_hbm, tile_vals, cotangent,
    output_hbm, grad_hbm,
    output, grad_weight, tile_count, features, send_rows, hub_owner, hub_row, row_list, vals, cot, source, stage, picked, ints, ints_smem,
    border_out, border_in, hub_out, hub_z, hub_part, hub_x, weight_t,
    core_out, core_in, y_out, y_in, sized, z_out, z_in, last_in,
    local_sems, send_sems, recv_sems,
):
    dom, feat = lax.axis_index("dom"), lax.axis_index("feat")
    z, x = dom // N_X, dom % N_X
    y, core = feat // 2, feat % 2

    def dom_far(i, dx):
        return lax.rem(z + far_first(i, N_Z), N_Z) * N_X + lax.rem(x + dx, N_X)

    def feat_far(i):
        t = N_FEAT - 2 - i
        j = (1 - t % 2) * (t // 2 + 1) + (t % 2) * (N_FEAT - 1 - t // 2)
        return lax.rem(feat + j, N_FEAT)

    def remote(src, dst, which, device):
        return pltpu.make_async_remote_copy(
            src_ref=src, dst_ref=dst, send_sem=send_sems.at[which], recv_sem=recv_sems.at[which],
            device_id=device, device_id_type=pl.DeviceIdType.MESH,
        )

    def wait_all(ref, sem):
        pltpu.make_async_copy(ref, ref, sem).wait()

    def wait_most(ref, sem):
        flat = sized.at[pl.ds(0, N_Y * N_X - 1)]
        wait_all(flat, sem)

    def fetch(src, dst, which):
        copy = pltpu.make_async_copy(src, dst, local_sems.at[which])
        copy.start()
        return copy

    barrier = pltpu.get_barrier_semaphore()
    each_dom(lambda i, dx: pl.semaphore_signal(
        barrier, inc=1, device_id={"dom": dom_far(i, dx)}, device_id_type=pl.DeviceIdType.MESH))
    loop(0, N_FEAT - 1, lambda i: pl.semaphore_signal(
        barrier, inc=1, device_id={"feat": feat_far(i)}, device_id_type=pl.DeviceIdType.MESH))

    owner_copy = fetch(hub_owner_hbm, hub_owner, 5)
    hub_row_copy = fetch(hub_row_hbm, hub_row, 6)
    features_copy = fetch(features_hbm, features, 3)
    rows_copy = fetch(send_rows_hbm, send_rows, 4)
    weight_copy = fetch(weight_hbm, weight_t.at[y, core], 7)
    count_copy = fetch(tile_count_hbm, tile_count, 8)
    vals_copy = fetch(tile_vals, vals, 0)
    cot_copy = fetch(cotangent, cot, 1)

    lane8 = lax.broadcasted_iota(I32, (8, TILE), 1)
    row8 = lax.broadcasted_iota(I32, (8, TILE), 0)

    features_copy.wait()
    for t in range(OWN):
        source[t] = features[:, t * TILE : (t + 1) * TILE]
    lane1 = lax.broadcasted_iota(I32, (1, TILE), 1)
    listed = jnp.zeros((1, TILE), I32)
    for k in range(SLOTS):
        listed = jnp.where(lane1 == k, tile_src[0, k], listed)
    ints[pl.ds(feat, 1)] = listed[None]

    owner_copy.wait()
    hub_row_copy.wait()
    owner = hub_owner[...].reshape(1, HUBS)
    earlier = (lax.broadcasted_iota(I32, (HUBS, HUBS), 0) < lax.broadcasted_iota(I32, (HUBS, HUBS), 1))
    owned = (lax.broadcasted_iota(I32, (N_DOM, HUBS), 0) == owner).astype(F32)
    before = jnp.dot(owned.astype(BF16), earlier.astype(F32).astype(BF16), preferred_element_type=F32)
    rank = jnp.dot(jnp.ones((8, N_DOM), BF16), (owned * before).astype(BF16), preferred_element_type=F32)
    rank = rank.astype(I32)
    mine = owner == dom
    place = lax.broadcasted_iota(I32, (TILE, HUBS), 0) % 64
    chosen = (mine & (rank[0:1] == place)).astype(F32).astype(BF16)
    row = hub_row[...].reshape(1, HUBS)
    row_parts = jnp.concatenate([jnp.broadcast_to(row // 16, (8, HUBS)), jnp.broadcast_to(row % 16, (8, HUBS))], axis=0)
    my_rows = lax.dot_general(
        row_parts.astype(F32).astype(BF16), chosen, (((1,), (1,)), ((), ())), preferred_element_type=F32
    )
    my_rows = my_rows[0:8].astype(I32) * 16 + my_rows[8:16].astype(I32)

    def columns(v, index):
        low, high = index % TILE, index // TILE
        found = jnp.zeros((8, TILE), F32)
        for t in range(OWN):
            part = pick(features[8 * v : 8 * v + 8, t * TILE : (t + 1) * TILE], low)
            found = jnp.where(high == t, part, found)
        return found

    hub_out[...] = jnp.where(lane8 < 64, columns(0, my_rows), columns(1, my_rows))

    rows_copy.wait()
    repeat = lax.broadcasted_iota(I32, (SEND, TILE), 1) % SEND == lax.broadcasted_iota(I32, (SEND, TILE), 0)
    row_list[...] = lax.dot_general(
        send_rows[...].astype(F32), repeat.astype(F32), (((0,), (0,)), ((), ())),
        precision=lax.Precision.HIGHEST, preferred_element_type=F32,
    ).astype(I32)

    group4 = lax.broadcasted_iota(I32, (4, TILE), 1) // 32
    in_group = [group4 == (t + x) % 4 for t in range(4)]

    def border_tile(q):
        lists = [jnp.broadcast_to(row_list[pl.ds(4 * q + d, 1), :], (8, TILE)) for d in range(4)]
        quarter = []
        for v in range(2):
            turned = lists[0]
            for d in range(1, 4):
                turned = jnp.where(lane8 // 32 == (d + 2 * v + row8 // 4 + x) % 4, lists[d], turned)
            found = columns(v, turned)
            quarter += [found[0:4], found[4:8]]
        for d in range(4):
            message = quarter[0]
            for a in range(4):
                message = jnp.where(in_group[(a + d) % 4], quarter[a], message)
            border_out[pl.ds(4 * q + d, 1)] = message[None]

    loop(0, BORDER, border_tile)

    weight_copy.wait()
    pl.semaphore_wait(barrier, N_DOM - 1 + N_FEAT - 1)

    def z_device(z_to):
        return {"dom": z_to * N_X + x}

    def x_device(x_to):
        return {"dom": z * N_X + x_to}

    def y_device(y_to):
        return {"feat": y_to * 2 + core}

    loop(0, N_Z - 1, lambda i: remote(
        hub_out, hub_z.at[z], 0, z_device(lax.rem(z + far_first(i, N_Z), N_Z))).start())
    each_dom(lambda i, dx: remote(
        border_out.at[dom_far(i, dx)], border_in.at[dom], 1, {"dom": dom_far(i, dx)}).start())
    loop(0, N_FEAT - 1, lambda i: remote(ints.at[feat], ints.at[feat], 2, {"feat": feat_far(i)}).start())
    loop(0, N_FEAT - 1, lambda i: remote(
        source.at[feat_far(i)], picked.at[0, feat], 3, {"feat": feat_far(i)}).start())
    loop(0, N_Y - 1, lambda i: remote(
        weight_t.at[y, core], weight_t.at[y, core], 4, y_device(lax.rem(y + far_first(i, N_Y), N_Y))).start())

    picked[0, pl.ds(feat, 1)] = source[pl.ds(feat, 1)]
    border_in[pl.ds(dom, 1)] = border_out[pl.ds(dom, 1)]
    hub_z[pl.ds(z, 1)] = hub_out[...][None]

    wait_all(hub_z.at[pl.ds(0, N_Z - 1)], recv_sems.at[0])
    owner8 = jnp.broadcast_to(owner, (8, HUBS))
    at = (owner8 // N_X % 2) * 64 + rank
    pair = jnp.where(owner8 % N_X == x, owner8 // (2 * N_X), N_Z)
    found = [jnp.zeros((8, TILE), F32)] * (2 * HUB_TILES)
    for p in range(N_Z // 2):
        even, odd = hub_z[2 * p], hub_z[2 * p + 1]
        tables = (
            jnp.where(lane8 < 64, even, pltpu.roll(odd, 64, 1)),
            jnp.where(lane8 < 64, pltpu.roll(even, 64, 1), odd),
        )
        for q in range(HUB_TILES):
            span = slice(q * TILE, (q + 1) * TILE)
            for v in range(2):
                found[2 * q + v] = jnp.where(pair[:, span] == p, pick(tables[v], at[:, span]), found[2 * q + v])
    for q in range(HUB_TILES):
        for v in range(2):
            hub_part[q, 8 * v : 8 * v + 8] = found[2 * q + v]
    loop(1, N_X, lambda j: remote(hub_part, hub_x.at[x], 5, x_device(lax.rem(x + j, N_X))).start())
    hub_x[pl.ds(x, 1)] = hub_part[...][None]

    wait_all(ints.at[pl.ds(0, N_FEAT - 1)], recv_sems.at[2])
    ints_copy = pltpu.make_async_copy(ints, ints_smem, local_sems.at[2])
    ints_copy.start()

    wait_all(border_in.at[pl.ds(0, N_DOM - 1)], recv_sems.at[1])
    quarter_of = [2 * v + row8 // 4 for v in range(2)]

    def border_arrived(q):
        pieces = []
        for e in range(4):
            piece = border_in[pl.ds(4 * q + e, 1)][0]
            pieces.append(jnp.concatenate([piece, piece], axis=0))
        for v in range(2):
            mixed = pieces[0]
            for e in range(1, 4):
                mixed = jnp.where(lane8 // 32 == (quarter_of[v] + e + x) % 4, pieces[e], mixed)
            source[pl.ds(OWN + q, 1), 8 * v : 8 * v + 8] = pick(mixed, (lane8 + 32 * (quarter_of[v] + x)) % TILE)[None]

    loop(0, BORDER, border_arrived)

    ints_copy.wait()

    def send_slots(first, last, which):
        def to_peer(i):
            peer = feat_far(i)
            for k in range(first, last):
                stage[peer, k] = source[ints_smem[peer, 0, k]]
            some = pl.ds(first, last - first)
            remote(stage.at[peer, some], picked.at[some, feat], which, {"feat": peer}).start()

        loop(0, N_FEAT - 1, to_peer)
        for k in range(first, last):
            picked[k, feat] = source[tile_src[0, k]]

    send_slots(1, 2, 6)
    wait_all(hub_x.at[pl.ds(0, N_X - 1)], recv_sems.at[5])
    for q in range(HUB_TILES):
        source[OWN + BORDER + q] = (hub_x[0, q] + hub_x[1, q]) + (hub_x[2, q] + hub_x[3, q])
    send_slots(2, 4, 7)
    send_slots(4, SLOTS, 10)
    wait_all(weight_t.at[pl.ds(0, N_Y - 1), 0], recv_sems.at[4])
    other = 1 - core
    weight_on = remote(weight_t.at[:, core], weight_t.at[:, core], 12, {"feat": y * 2 + other})
    weight_on.start()

    vals_copy.wait()
    count_copy.wait()
    count = tile_count[0]

    def aggregate(k):
        live = jnp.where(k < count, 1.0, 0.0).astype(F32)
        return dot3(picked[k].reshape(D, TILE), vals[0, k] * live, ((1,), (0,)))

    def arrived(first, last, which):
        wait_all(picked.at[pl.ds(first, last - first), pl.ds(0, N_FEAT - 1)], recv_sems.at[which])

    arrived(0, 1, 3)
    aggregated = aggregate(0)
    for first, last, which in ((1, 2, 6), (2, 4, 7), (4, SLOTS, 10)):
        if last == SLOTS:
            weight_on.wait_recv()
            cot_copy.wait()
        arrived(first, last, which)
        for k in range(first, last):
            aggregated += aggregate(k)

    result = jnp.tanh(dot3(weight_t[...].reshape(D, D), aggregated, ((1,), (0,))))
    output[...] = result
    output_copy = fetch(output, output_hbm, 9)
    pre_grad = cot[...] * (1.0 - result * result)
    partial = dot3(pre_grad, aggregated, ((1,), (1,)))

    for c in range(2):
        for w in range(N_Y):
            for j in range(N_X):
                top, left = SHARE * (2 * w + c) + 8 * (j // 2), TILE * (j % 2)
                core_out[c, w, j] = partial[top : top + 8, left : left + TILE]
    to_core = remote(core_out.at[other], core_in, 8, {"feat": y * 2 + other})
    to_core.start()
    to_core.wait_recv()
    y_out[...] = core_out[core] + core_in[...]

    def to_column(i, dx):
        y_to, x_to = lax.rem(y + far_first(i, N_Y), N_Y), lax.rem(x + dx, N_X)
        device = {"dom": z * N_X + x_to, "feat": y_to * 2 + core}
        remote(y_out.at[y_to, x_to], y_in.at[y, x], 9, device).start()

    def of_y(i):
        for dx in (2, 1, 3, 0):
            to_column(i, dx)

    loop(0, N_Y - 1, of_y)
    for dx in (2, 1, 3):
        to_column(N_Y - 1, dx)
    y_in[pl.ds(y, 1), pl.ds(x, 1)] = y_out[pl.ds(y, 1), pl.ds(x, 1)]
    wait_most(y_in, recv_sems.at[9])
    total = [y_in[w, 0] + y_in[w, 1] + (y_in[w, 2] + y_in[w, 3]) for w in range(N_Y)]
    while len(total) > 1:
        total = [a + b for a, b in zip(total[0::2], total[1::2])]
    z_out[...] = total[0]
    loop(0, N_Z - 1, lambda i: remote(
        z_out, z_in.at[z], 11, z_device(lax.rem(z + far_first(i, N_Z), N_Z))).start())
    z_in[pl.ds(z, 1)] = z_out[...][None]
    wait_all(z_in.at[pl.ds(0, N_Z - 1)], recv_sems.at[11])
    thirds = [z_in[w] + z_in[w + 1] + (z_in[w + 2] + z_in[w + 3]) for w in range(0, N_Z, 4)]
    chunk = thirds[0] + thirds[1] + thirds[2]
    last_in[pl.ds(x, 1)] = chunk[None]
    loop(1, N_X, lambda j: remote(last_in.at[x], last_in.at[x], 13, x_device(lax.rem(x + j, N_X))).start())
    wait_all(last_in.at[pl.ds(0, N_X - 1)], recv_sems.at[13])
    whole = jnp.concatenate(
        [jnp.concatenate([last_in[0], last_in[1]], axis=1), jnp.concatenate([last_in[2], last_in[3]], axis=1)], axis=0
    )
    grad_weight[...] = whole
    fetch(grad_weight, grad_hbm, 10).wait()
    output_copy.wait()

    wait_all(hub_z.at[pl.ds(0, N_Z - 1)], send_sems.at[0])
    wait_all(border_in.at[pl.ds(0, N_DOM - 1)], send_sems.at[1])
    wait_all(ints.at[pl.ds(0, N_FEAT - 1)], send_sems.at[2])
    wait_all(picked.at[0, pl.ds(0, N_FEAT - 1)], send_sems.at[3])
    wait_all(weight_t.at[pl.ds(0, N_Y - 1), 0], send_sems.at[4])
    wait_all(hub_x.at[pl.ds(0, N_X - 1)], send_sems.at[5])
    for first, last, which in ((1, 2, 6), (2, 4, 7), (4, SLOTS, 10)):
        wait_all(picked.at[pl.ds(first, last - first), pl.ds(0, N_FEAT - 1)], send_sems.at[which])
    weight_on.wait_send()
    to_core.wait_send()
    wait_most(y_in, send_sems.at[9])
    wait_all(z_in.at[pl.ds(0, N_Z - 1)], send_sems.at[11])
    wait_all(last_in.at[pl.ds(0, N_X - 1)], send_sems.at[13])


def hand_on(output, grad_weight, output_to, grad_to, held, held_grad, sems):
    ways = ((output, held, output_to), (grad_weight, held_grad, grad_to))
    incoming = [pltpu.make_async_copy(w[0], w[1], sems.at[i]) for i, w in enumerate(ways)]
    outgoing = [pltpu.make_async_copy(w[1], w[2], sems.at[2 + i]) for i, w in enumerate(ways)]
    for copy in incoming:
        copy.start()
    for copy, onward in zip(incoming, outgoing):
        copy.wait()
        onward.start()
    for copy in outgoing:
        copy.wait()


def on_device(
    features, tile_vals, tile_src, tile_count, send_rows, hub_owner, hub_row, weight, cotangent
):
    smem = pl.BlockSpec(memory_space=pltpu.SMEM)
    hbm = pl.BlockSpec(memory_space=pltpu.HBM)
    scratch = [
        pltpu.VMEM(cotangent.shape, F32),
        pltpu.VMEM((SHARE, D), F32),
        pltpu.SMEM(tile_count.shape, I32),
        pltpu.VMEM(features.shape, F32),
        pltpu.VMEM((SEND, N_DOM), I32),
        pltpu.VMEM((HUBS,), I32),
        pltpu.VMEM((HUBS,), I32),
        pltpu.VMEM((N_DOM, TILE), I32),
        pltpu.VMEM(tile_vals.shape, F32),
        pltpu.VMEM(cotangent.shape, F32),
        pltpu.VMEM((EXT, SHARE, TILE), F32),
        pltpu.VMEM((N_FEAT, SLOTS, SHARE, TILE), F32),
        pltpu.VMEM((SLOTS, N_FEAT, SHARE, TILE), F32),
        pltpu.VMEM((N_FEAT, 1, TILE), I32),
        pltpu.SMEM((N_FEAT, 1, TILE), I32),
        pltpu.VMEM((N_DOM, 4, TILE), F32),
        pltpu.VMEM((N_DOM, 4, TILE), F32),
        pltpu.VMEM((8, TILE), F32),
        pltpu.VMEM((N_Z, 8, TILE), F32),
        pltpu.VMEM((HUB_TILES, SHARE, TILE), F32),
        pltpu.VMEM((N_X, HUB_TILES, SHARE, TILE), F32),
        pltpu.VMEM((N_Y, 2, SHARE, D), F32),
        pltpu.VMEM((2, N_Y, N_X, 8, TILE), F32),
        pltpu.VMEM((N_Y, N_X, 8, TILE), F32),
        pltpu.VMEM((N_Y, N_X, 8, TILE), F32),
        pltpu.VMEM((N_Y, N_X, 8, TILE), F32),
        pltpu.VMEM((N_Y * N_X, 8, TILE), F32),
        pltpu.VMEM((8, TILE), F32),
        pltpu.VMEM((N_Z, 8, TILE), F32),
        pltpu.VMEM((N_X, 8, TILE), F32),
        pltpu.SemaphoreType.DMA((11,)),
        pltpu.SemaphoreType.DMA((14,)),
        pltpu.SemaphoreType.DMA((14,)),
    ]
    results = (
        jax.ShapeDtypeStruct(cotangent.shape, F32),
        jax.ShapeDtypeStruct((SHARE, D), F32),
    )
    made = pl.pallas_call(
        kernel,
        out_shape=results,
        in_specs=[smem] + [hbm] * 8,
        out_specs=(hbm, hbm),
        scratch_shapes=scratch,
        compiler_params=pltpu.CompilerParams(
            collective_id=0, has_side_effects=True, vmem_limit_bytes=60 * 1024 * 1024
        ),
    )(
        tile_src, tile_count, features, send_rows.T, hub_owner, hub_row, weight.T, tile_vals, cotangent
    )
    output, grad_weight = pl.pallas_call(
        hand_on,
        out_shape=results,
        in_specs=[hbm, hbm],
        out_specs=(hbm, hbm),
        scratch_shapes=[pltpu.VMEM(r.shape, F32) for r in results] + [pltpu.SemaphoreType.DMA((4,))],
        compiler_params=pltpu.CompilerParams(vmem_limit_bytes=60 * 1024 * 1024),
    )(*made)
    return output, grad_weight.T


def solution(mesh):
    in_specs = (
        P("feat", "dom"),
        P(("dom", "feat"), None, None, None),
        P(("dom", "feat"), None),
        P(("dom", "feat")),
        P("dom", None),
        P(),
        P(),
        P(None, "feat"),
        P(None, ("dom", "feat")),
    )
    out_specs = (P(None, ("dom", "feat")), P(None, "feat"))
    return jax.shard_map(
        on_device, mesh=mesh, in_specs=in_specs, out_specs=out_specs, check_vma=False
    )
```

```python
import jax
import jax.numpy as jnp
from jax import lax
from jax.experimental import pallas as pl
from jax.experimental.pallas import tpu as pltpu
from jax.sharding import PartitionSpec as P

N_X, N_Z, N_Y = 4, 12, 8
N_DOM = N_X * N_Z
N_FEAT = 2 * N_Y
D = 256
TILE = 128
SHARE = D // N_FEAT
SEND = 32
SLOTS = 6
OWN = 16
BORDER = 12
HUB_TILES = 6
HUBS = HUB_TILES * TILE
EXT = OWN + BORDER + HUB_TILES
F32, BF16, I32 = jnp.float32, jnp.bfloat16, jnp.int32


def split(value):
    high = value.astype(BF16)
    return high, (value - high.astype(F32)).astype(BF16)


def product(a, b, dims):
    def one(u, v):
        return lax.dot_general(u, v, (dims, ((), ())), preferred_element_type=F32)

    return one(a[0], b[0]) + (one(a[0], b[1]) + one(a[1], b[0]))


def pick(table, index):
    return jnp.take_along_axis(table, index, axis=1, mode="promise_in_bounds")


def loop(first, last, body):
    def step(i, carry):
        body(i)
        return carry

    lax.fori_loop(first, last, step, 0)


def far_first(i, n):
    return n // 2 + (i % 2) * ((i + 1) // 2) - (1 - i % 2) * (i // 2)


def each_dom(body):
    def of_z(i):
        for dx in (2, 1, 3, 0):
            body(i, dx)

    loop(0, N_Z - 1, of_z)
    for dx in (2, 1, 3):
        body(N_Z - 1, dx)


def kernel(
    tile_src_hbm, tile_count_hbm, features_hbm, send_rows_hbm, hub_owner_hbm, hub_row_hbm, weight_hbm, tile_vals, cotangent,
    output_hbm, grad_hbm,
    output, grad_weight, tile_src, tile_count, features, send_rows, hub_owner, hub_row, row_list, vals, vals_high, vals_low, cot, pre_grad, source, stage, picked, ints, ints_smem,
    border_out, border_in, hub_out, hub_z, hub_part, hub_x, weight_t,
    core_out, core_in, y_out, y_in, sized, z_out, z_in, last_in,
    local_sems, send_sems, recv_sems,
):
    dom, feat = lax.axis_index("dom"), lax.axis_index("feat")
    z, x = dom // N_X, dom % N_X
    y, core = feat // 2, feat % 2

    def dom_far(i, dx):
        return lax.rem(z + far_first(i, N_Z), N_Z) * N_X + lax.rem(x + dx, N_X)

    def feat_far(i):
        t = N_FEAT - 2 - i
        j = (1 - t % 2) * (t // 2 + 1) + (t % 2) * (N_FEAT - 1 - t // 2)
        return lax.rem(feat + j, N_FEAT)

    def remote(src, dst, which, device):
        return pltpu.make_async_remote_copy(
            src_ref=src, dst_ref=dst, send_sem=send_sems.at[which], recv_sem=recv_sems.at[which],
            device_id=device, device_id_type=pl.DeviceIdType.MESH,
        )

    def wait_all(ref, sem):
        pltpu.make_async_copy(ref, ref, sem).wait()

    def wait_most(ref, sem):
        flat = sized.at[pl.ds(0, N_Y * N_X - 1)]
        wait_all(flat, sem)

    def fetch(src, dst, which):
        copy = pltpu.make_async_copy(src, dst, local_sems.at[which])
        copy.start()
        return copy

    barrier = pltpu.get_barrier_semaphore()
    each_dom(lambda i, dx: pl.semaphore_signal(
        barrier, inc=1, device_id={"dom": dom_far(i, dx)}, device_id_type=pl.DeviceIdType.MESH))
    loop(0, N_FEAT - 1, lambda i: pl.semaphore_signal(
        barrier, inc=1, device_id={"feat": feat_far(i)}, device_id_type=pl.DeviceIdType.MESH))

    src_copy = fetch(tile_src_hbm, tile_src, 11)
    owner_copy = fetch(hub_owner_hbm, hub_owner, 5)
    hub_row_copy = fetch(hub_row_hbm, hub_row, 6)
    features_copy = fetch(features_hbm, features, 3)
    rows_copy = fetch(send_rows_hbm, send_rows, 4)
    weight_copy = fetch(weight_hbm, weight_t.at[y, core], 7)
    count_copy = fetch(tile_count_hbm, tile_count, 8)
    vals_copy = fetch(tile_vals, vals, 0)
    cot_copy = fetch(cotangent, cot, 1)

    lane8 = lax.broadcasted_iota(I32, (8, TILE), 1)
    row8 = lax.broadcasted_iota(I32, (8, TILE), 0)

    features_copy.wait()
    def columns(v, index):
        low, high = index % TILE, index // TILE
        found = jnp.zeros((8, TILE), F32)
        for t in range(OWN):
            part = pick(features[8 * v : 8 * v + 8, t * TILE : (t + 1) * TILE], low)
            found = jnp.where(high == t, part, found)
        return found

    rows_copy.wait()
    repeat = lax.broadcasted_iota(I32, (SEND, TILE), 1) % SEND == lax.broadcasted_iota(I32, (SEND, TILE), 0)
    row_list[...] = lax.dot_general(
        send_rows[...].astype(F32), repeat.astype(F32), (((0,), (0,)), ((), ())),
        precision=lax.Precision.HIGHEST, preferred_element_type=F32,
    ).astype(I32)

    group4 = lax.broadcasted_iota(I32, (4, TILE), 1) // 32
    in_group = [group4 == (t + x) % 4 for t in range(4)]

    def border_tile(q):
        lists = [jnp.broadcast_to(row_list[pl.ds(4 * q + d, 1), :], (8, TILE)) for d in range(4)]
        quarter = []
        for v in range(2):
            turned = lists[0]
            for d in range(1, 4):
                turned = jnp.where(lane8 // 32 == (d + 2 * v + row8 // 4 + x) % 4, lists[d], turned)
            found = columns(v, turned)
            quarter += [found[0:4], found[4:8]]
        for d in range(4):
            message = quarter[0]
            for a in range(4):
                message = jnp.where(in_group[(a + d) % 4], quarter[a], message)
            border_out[pl.ds(4 * q + d, 1)] = message[None]

    loop(0, BORDER, border_tile)

    for t in range(OWN):
        source[t] = features[:, t * TILE : (t + 1) * TILE]
    lane1 = lax.broadcasted_iota(I32, (1, TILE), 1)
    src_copy.wait()
    listed = jnp.zeros((1, TILE), I32)
    for k in range(SLOTS):
        listed = jnp.where(lane1 == k, tile_src[0, k], listed)
    ints[pl.ds(feat, 1)] = listed[None]

    weight_copy.wait()
    pl.semaphore_wait(barrier, N_DOM - 1 + N_FEAT - 1)

    def z_device(z_to):
        return {"dom": z_to * N_X + x}

    def x_device(x_to):
        return {"dom": z * N_X + x_to}

    def y_device(y_to):
        return {"feat": y_to * 2 + core}

    each_dom(lambda i, dx: remote(
        border_out.at[dom_far(i, dx)], border_in.at[dom], 1, {"dom": dom_far(i, dx)}).start())
    owner_copy.wait()
    hub_row_copy.wait()
    owner = hub_owner[...].reshape(1, HUBS)
    earlier = (lax.broadcasted_iota(I32, (HUBS, HUBS), 0) < lax.broadcasted_iota(I32, (HUBS, HUBS), 1))
    owned = (lax.broadcasted_iota(I32, (N_DOM, HUBS), 0) == owner).astype(F32)
    before = jnp.dot(owned.astype(BF16), earlier.astype(F32).astype(BF16), preferred_element_type=F32)
    rank = jnp.dot(jnp.ones((8, N_DOM), BF16), (owned * before).astype(BF16), preferred_element_type=F32)
    rank = rank.astype(I32)
    mine = owner == dom
    place = lax.broadcasted_iota(I32, (TILE, HUBS), 0) % 64
    chosen = (mine & (rank[0:1] == place)).astype(F32).astype(BF16)
    row = hub_row[...].reshape(1, HUBS)
    row_parts = jnp.concatenate([jnp.broadcast_to(row // 16, (8, HUBS)), jnp.broadcast_to(row % 16, (8, HUBS))], axis=0)
    my_rows = lax.dot_general(
        row_parts.astype(F32).astype(BF16), chosen, (((1,), (1,)), ((), ())), preferred_element_type=F32
    )
    my_rows = my_rows[0:8].astype(I32) * 16 + my_rows[8:16].astype(I32)

    hub_out[...] = jnp.where(lane8 < 64, columns(0, my_rows), columns(1, my_rows))

    loop(0, N_Z - 1, lambda i: remote(
        hub_out, hub_z.at[z], 0, z_device(lax.rem(z + far_first(i, N_Z), N_Z))).start())
    loop(0, N_FEAT - 1, lambda i: remote(ints.at[feat], ints.at[feat], 2, {"feat": feat_far(i)}).start())
    loop(0, N_FEAT - 1, lambda i: remote(
        source.at[feat_far(i)], picked.at[0, feat], 3, {"feat": feat_far(i)}).start())
    loop(0, N_Y - 1, lambda i: remote(
        weight_t.at[y, core], weight_t.at[y, core], 4, y_device(lax.rem(y + far_first(i, N_Y), N_Y))).start())

    picked[0, pl.ds(feat, 1)] = source[pl.ds(feat, 1)]
    border_in[pl.ds(dom, 1)] = border_out[pl.ds(dom, 1)]
    hub_z[pl.ds(z, 1)] = hub_out[...][None]

    wait_all(hub_z.at[pl.ds(0, N_Z - 1)], recv_sems.at[0])
    owner8 = jnp.broadcast_to(owner, (8, HUBS))
    at = (owner8 // N_X % 2) * 64 + rank
    pair = jnp.where(owner8 % N_X == x, owner8 // (2 * N_X), N_Z)
    found = [jnp.zeros((8, TILE), F32)] * (2 * HUB_TILES)
    for p in range(N_Z // 2):
        even, odd = hub_z[2 * p], hub_z[2 * p + 1]
        tables = (
            jnp.where(lane8 < 64, even, pltpu.roll(odd, 64, 1)),
            jnp.where(lane8 < 64, pltpu.roll(even, 64, 1), odd),
        )
        for q in range(HUB_TILES):
            span = slice(q * TILE, (q + 1) * TILE)
            for v in range(2):
                found[2 * q + v] = jnp.where(pair[:, span] == p, pick(tables[v], at[:, span]), found[2 * q + v])
    for q in range(HUB_TILES):
        for v in range(2):
            hub_part[q, 8 * v : 8 * v + 8] = found[2 * q + v]
    loop(1, N_X, lambda j: remote(hub_part, hub_x.at[x], 5, x_device(lax.rem(x + j, N_X))).start())
    hub_x[pl.ds(x, 1)] = hub_part[...][None]

    wait_all(ints.at[pl.ds(0, N_FEAT - 1)], recv_sems.at[2])
    ints_copy = pltpu.make_async_copy(ints, ints_smem, local_sems.at[2])
    ints_copy.start()

    wait_all(border_in.at[pl.ds(0, N_DOM - 1)], recv_sems.at[1])
    quarter_of = [2 * v + row8 // 4 for v in range(2)]

    def border_arrived(q):
        pieces = []
        for e in range(4):
            piece = border_in[pl.ds(4 * q + e, 1)][0]
            pieces.append(jnp.concatenate([piece, piece], axis=0))
        for v in range(2):
            mixed = pieces[0]
            for e in range(1, 4):
                mixed = jnp.where(lane8 // 32 == (quarter_of[v] + e + x) % 4, pieces[e], mixed)
            source[pl.ds(OWN + q, 1), 8 * v : 8 * v + 8] = pick(mixed, (lane8 + 32 * (quarter_of[v] + x)) % TILE)[None]

    loop(0, BORDER, border_arrived)

    ints_copy.wait()

    def send_slots(first, last, which):
        def to_peer(i):
            peer = feat_far(i)
            for k in range(first, last):
                stage[peer, k] = source[ints_smem[peer, 0, k]]
            some = pl.ds(first, last - first)
            remote(stage.at[peer, some], picked.at[some, feat], which, {"feat": peer}).start()

        loop(0, N_FEAT - 1, to_peer)
        for k in range(first, last):
            picked[k, feat] = source[tile_src[0, k]]

    send_slots(1, 2, 6)
    wait_all(hub_x.at[pl.ds(0, N_X - 1)], recv_sems.at[5])
    for q in range(HUB_TILES):
        source[OWN + BORDER + q] = (hub_x[0, q] + hub_x[1, q]) + (hub_x[2, q] + hub_x[3, q])
    send_slots(2, 4, 7)
    send_slots(4, SLOTS, 10)
    wait_all(weight_t.at[pl.ds(0, N_Y - 1), 0], recv_sems.at[4])
    other = 1 - core
    weight_on = remote(weight_t.at[:, core], weight_t.at[:, core], 12, {"feat": y * 2 + other})
    weight_on.start()

    vals_copy.wait()
    count_copy.wait()
    count = tile_count[0]
    for k in range(SLOTS):
        live = jnp.where(k < count, 1.0, 0.0).astype(F32)
        vals_high[k], vals_low[k] = split(vals[0, k] * live)

    def aggregate(first, last, which):
        wait_all(picked.at[pl.ds(first, last - first), pl.ds(0, N_FEAT - 1)], recv_sems.at[which])
        taken = [picked[k].reshape(D, TILE) for k in range(first, last)]
        taken = split(jnp.concatenate(taken, axis=1))
        rows = (last - first) * TILE
        factor = (vals_high[first:last].reshape(rows, TILE), vals_low[first:last].reshape(rows, TILE))
        return product(taken, factor, ((1,), (0,)))

    aggregated = aggregate(0, 1, 3)
    aggregated += aggregate(1, 2, 6)
    weight_on.wait_recv()
    weight_parts = split(weight_t[...].reshape(D, D))
    cot_copy.wait()
    aggregated += aggregate(2, 4, 7)
    aggregated += aggregate(4, SLOTS, 10)
    parts = split(aggregated)
    result = jnp.tanh(product(weight_parts, parts, ((1,), (0,))))
    output[...] = result
    output_copy = fetch(output, output_hbm, 9)
    pre_grad[...] = (cot[...] * (1.0 - result * result)).reshape(pre_grad.shape)

    def gradient(c, to):
        partial = product(split(pre_grad[:, c].reshape(N_Y * SHARE, TILE)), parts, ((1,), (1,)))
        for w in range(N_Y):
            for j in range(N_X):
                top, left = SHARE * w + 8 * (j // 2), TILE * (j % 2)
                to[w, j] = partial[top : top + 8, left : left + TILE]

    gradient(other, core_out)
    to_core = remote(core_out, core_in, 8, {"feat": y * 2 + other})
    to_core.start()
    gradient(core, y_out)
    to_core.wait_recv()
    y_out[...] += core_in[...]

    def to_column(i, dx):
        y_to, x_to = lax.rem(y + far_first(i, N_Y), N_Y), lax.rem(x + dx, N_X)
        device = {"dom": z * N_X + x_to, "feat": y_to * 2 + core}
        remote(y_out.at[y_to, x_to], y_in.at[y, x], 9, device).start()

    def of_y(i):
        for dx in (2, 1, 3, 0):
            to_column(i, dx)

    loop(0, N_Y - 1, of_y)
    for dx in (2, 1, 3):
        to_column(N_Y - 1, dx)
    y_in[pl.ds(y, 1), pl.ds(x, 1)] = y_out[pl.ds(y, 1), pl.ds(x, 1)]
    wait_most(y_in, recv_sems.at[9])
    total = [y_in[w, 0] + y_in[w, 1] + (y_in[w, 2] + y_in[w, 3]) for w in range(N_Y)]
    while len(total) > 1:
        total = [a + b for a, b in zip(total[0::2], total[1::2])]
    z_out[...] = total[0]
    loop(0, N_Z - 1, lambda i: remote(
        z_out, z_in.at[z], 11, z_device(lax.rem(z + far_first(i, N_Z), N_Z))).start())
    z_in[pl.ds(z, 1)] = z_out[...][None]
    wait_all(z_in.at[pl.ds(0, N_Z - 1)], recv_sems.at[11])
    thirds = [z_in[w] + z_in[w + 1] + (z_in[w + 2] + z_in[w + 3]) for w in range(0, N_Z, 4)]
    chunk = thirds[0] + thirds[1] + thirds[2]
    last_in[pl.ds(x, 1)] = chunk[None]
    loop(1, N_X, lambda j: remote(last_in.at[x], last_in.at[x], 13, x_device(lax.rem(x + j, N_X))).start())
    wait_all(last_in.at[pl.ds(0, N_X - 1)], recv_sems.at[13])
    whole = jnp.concatenate(
        [jnp.concatenate([last_in[0], last_in[1]], axis=1), jnp.concatenate([last_in[2], last_in[3]], axis=1)], axis=0
    )
    grad_weight[...] = whole
    fetch(grad_weight, grad_hbm, 10).wait()
    output_copy.wait()

    wait_all(hub_z.at[pl.ds(0, N_Z - 1)], send_sems.at[0])
    wait_all(border_in.at[pl.ds(0, N_DOM - 1)], send_sems.at[1])
    wait_all(ints.at[pl.ds(0, N_FEAT - 1)], send_sems.at[2])
    wait_all(picked.at[0, pl.ds(0, N_FEAT - 1)], send_sems.at[3])
    wait_all(weight_t.at[pl.ds(0, N_Y - 1), 0], send_sems.at[4])
    wait_all(hub_x.at[pl.ds(0, N_X - 1)], send_sems.at[5])
    for first, last, which in ((1, 2, 6), (2, 4, 7), (4, SLOTS, 10)):
        wait_all(picked.at[pl.ds(first, last - first), pl.ds(0, N_FEAT - 1)], send_sems.at[which])
    weight_on.wait_send()
    to_core.wait_send()
    wait_most(y_in, send_sems.at[9])
    wait_all(z_in.at[pl.ds(0, N_Z - 1)], send_sems.at[11])
    wait_all(last_in.at[pl.ds(0, N_X - 1)], send_sems.at[13])


def hand_on(output, grad_weight, output_to, grad_to, held, held_grad, sems):
    ways = ((output, held, output_to), (grad_weight, held_grad, grad_to))
    incoming = [pltpu.make_async_copy(w[0], w[1], sems.at[i]) for i, w in enumerate(ways)]
    outgoing = [pltpu.make_async_copy(w[1], w[2], sems.at[2 + i]) for i, w in enumerate(ways)]
    for copy in incoming:
        copy.start()
    for copy, onward in zip(incoming, outgoing):
        copy.wait()
        onward.start()
    for copy in outgoing:
        copy.wait()


def on_device(
    features, tile_vals, tile_src, tile_count, send_rows, hub_owner, hub_row, weight, cotangent
):
    hbm = pl.BlockSpec(memory_space=pltpu.HBM)
    scratch = [
        pltpu.VMEM(cotangent.shape, F32),
        pltpu.VMEM((SHARE, D), F32),
        pltpu.SMEM(tile_src.shape, I32),
        pltpu.SMEM(tile_count.shape, I32),
        pltpu.VMEM(features.shape, F32),
        pltpu.VMEM((SEND, N_DOM), I32),
        pltpu.VMEM((HUBS,), I32),
        pltpu.VMEM((HUBS,), I32),
        pltpu.VMEM((N_DOM, TILE), I32),
        pltpu.VMEM(tile_vals.shape, F32),
        pltpu.VMEM((SLOTS, TILE, TILE), BF16),
        pltpu.VMEM((SLOTS, TILE, TILE), BF16),
        pltpu.VMEM(cotangent.shape, F32),
        pltpu.VMEM((N_Y, 2, SHARE, TILE), F32),
        pltpu.VMEM((EXT, SHARE, TILE), F32),
        pltpu.VMEM((N_FEAT, SLOTS, SHARE, TILE), F32),
        pltpu.VMEM((SLOTS, N_FEAT, SHARE, TILE), F32),
        pltpu.VMEM((N_FEAT, 1, TILE), I32),
        pltpu.SMEM((N_FEAT, 1, TILE), I32),
        pltpu.VMEM((N_DOM, 4, TILE), F32),
        pltpu.VMEM((N_DOM, 4, TILE), F32),
        pltpu.VMEM((8, TILE), F32),
        pltpu.VMEM((N_Z, 8, TILE), F32),
        pltpu.VMEM((HUB_TILES, SHARE, TILE), F32),
        pltpu.VMEM((N_X, HUB_TILES, SHARE, TILE), F32),
        pltpu.VMEM((N_Y, 2, SHARE, D), F32),
        pltpu.VMEM((N_Y, N_X, 8, TILE), F32),
        pltpu.VMEM((N_Y, N_X, 8, TILE), F32),
        pltpu.VMEM((N_Y, N_X, 8, TILE), F32),
        pltpu.VMEM((N_Y, N_X, 8, TILE), F32),
        pltpu.VMEM((N_Y * N_X, 8, TILE), F32),
        pltpu.VMEM((8, TILE), F32),
        pltpu.VMEM((N_Z, 8, TILE), F32),
        pltpu.VMEM((N_X, 8, TILE), F32),
        pltpu.SemaphoreType.DMA((12,)),
        pltpu.SemaphoreType.DMA((14,)),
        pltpu.SemaphoreType.DMA((14,)),
    ]
    results = (
        jax.ShapeDtypeStruct(cotangent.shape, F32),
        jax.ShapeDtypeStruct((SHARE, D), F32),
    )
    made = pl.pallas_call(
        kernel,
        out_shape=results,
        in_specs=[hbm] * 9,
        out_specs=(hbm, hbm),
        scratch_shapes=scratch,
        compiler_params=pltpu.CompilerParams(
            collective_id=0, has_side_effects=True, vmem_limit_bytes=60 * 1024 * 1024
        ),
    )(
        tile_src, tile_count, features, send_rows.T, hub_owner, hub_row, weight.T, tile_vals, cotangent
    )
    output, grad_weight = pl.pallas_call(
        hand_on,
        out_shape=results,
        in_specs=[hbm, hbm],
        out_specs=(hbm, hbm),
        scratch_shapes=[pltpu.VMEM(r.shape, F32) for r in results] + [pltpu.SemaphoreType.DMA((4,))],
        compiler_params=pltpu.CompilerParams(vmem_limit_bytes=60 * 1024 * 1024),
    )(*made)
    return output, grad_weight.T


def solution(mesh):
    in_specs = (
        P("feat", "dom"),
        P(("dom", "feat"), None, None, None),
        P(("dom", "feat"), None),
        P(("dom", "feat")),
        P("dom", None),
        P(),
        P(),
        P(None, "feat"),
        P(None, ("dom", "feat")),
    )
    out_specs = (P(None, ("dom", "feat")), P(None, "feat"))
    return jax.shard_map(
        on_device, mesh=mesh, in_specs=in_specs, out_specs=out_specs, check_vma=False
    )
```

```python
import jax
import jax.numpy as jnp
from jax import lax
from jax.experimental import pallas as pl
from jax.experimental.pallas import tpu as pltpu
from jax.sharding import PartitionSpec as P

N_X, N_Z, N_Y = 4, 12, 8
N_DOM = N_X * N_Z
N_FEAT = 2 * N_Y
D = 256
TILE = 128
SHARE = D // N_FEAT
SEND = 32
SLOTS = 6
OWN = 16
BORDER = 12
HUB_TILES = 6
HUBS = HUB_TILES * TILE
EXT = OWN + BORDER + HUB_TILES
F32, BF16, I32 = jnp.float32, jnp.bfloat16, jnp.int32


def split(value):
    high = value.astype(BF16)
    return high, (value - high.astype(F32)).astype(BF16)


def product(a, b, dims):
    def one(u, v):
        return lax.dot_general(u, v, (dims, ((), ())), preferred_element_type=F32)

    return one(a[0], b[0]) + (one(a[0], b[1]) + one(a[1], b[0]))


def pick(table, index):
    return jnp.take_along_axis(table, index, axis=1, mode="promise_in_bounds")


def loop(first, last, body):
    def step(i, carry):
        body(i)
        return carry

    lax.fori_loop(first, last, step, 0)


def far_first(i, n):
    return n // 2 + (i % 2) * ((i + 1) // 2) - (1 - i % 2) * (i // 2)


def each_dom(body):
    def hops(at):
        dz = far_first(at[0], N_Z)
        return min(dz, N_Z - dz) + min(at[1], N_X - at[1])

    offsets = [(i, dx) for i in range(N_Z) for dx in (2, 1, 3, 0)][:-1]
    for i, dx in sorted(offsets, key=hops, reverse=True):
        body(i, dx)


def kernel(
    tile_src_hbm, tile_count_hbm, features_hbm, send_rows_hbm, hub_owner_hbm, hub_row_hbm, weight_hbm, tile_vals, cotangent,
    output_hbm, grad_hbm,
    output, grad_weight, tile_src, tile_count, features, send_rows, hub_owner, hub_row, row_list, vals, vals_high, vals_low, cot, pre_grad, source, stage, picked, ints, ints_smem,
    border_out, border_in, hub_out, hub_z, hub_part, hub_x, weight_t,
    core_out, core_in, y_out, y_in, sized, z_out, z_in, last_in,
    local_sems, send_sems, recv_sems,
):
    dom, feat = lax.axis_index("dom"), lax.axis_index("feat")
    z, x = dom // N_X, dom % N_X
    y, core = feat // 2, feat % 2

    def dom_far(i, dx):
        return lax.rem(z + far_first(i, N_Z), N_Z) * N_X + lax.rem(x + dx, N_X)

    def feat_far(i):
        t = N_FEAT - 2 - i
        j = (1 - t % 2) * (t // 2 + 1) + (t % 2) * (N_FEAT - 1 - t // 2)
        return lax.rem(feat + j, N_FEAT)

    def remote(src, dst, which, device):
        return pltpu.make_async_remote_copy(
            src_ref=src, dst_ref=dst, send_sem=send_sems.at[which], recv_sem=recv_sems.at[which],
            device_id=device, device_id_type=pl.DeviceIdType.MESH,
        )

    def wait_all(ref, sem):
        pltpu.make_async_copy(ref, ref, sem).wait()

    def wait_most(ref, sem):
        flat = sized.at[pl.ds(0, N_Y * N_X - 1)]
        wait_all(flat, sem)

    def fetch(src, dst, which):
        copy = pltpu.make_async_copy(src, dst, local_sems.at[which])
        copy.start()
        return copy

    barrier = pltpu.get_barrier_semaphore()
    each_dom(lambda i, dx: pl.semaphore_signal(
        barrier, inc=1, device_id={"dom": dom_far(i, dx)}, device_id_type=pl.DeviceIdType.MESH))
    loop(0, N_FEAT - 1, lambda i: pl.semaphore_signal(
        barrier, inc=1, device_id={"feat": feat_far(i)}, device_id_type=pl.DeviceIdType.MESH))

    src_copy = fetch(tile_src_hbm, tile_src, 11)
    owner_copy = fetch(hub_owner_hbm, hub_owner, 5)
    hub_row_copy = fetch(hub_row_hbm, hub_row, 6)
    features_copy = fetch(features_hbm, features, 3)
    rows_copy = fetch(send_rows_hbm, send_rows, 4)
    weight_copy = fetch(weight_hbm, weight_t.at[y, core], 7)
    count_copy = fetch(tile_count_hbm, tile_count, 8)
    vals_copy = fetch(tile_vals, vals, 0)
    cot_copy = fetch(cotangent, cot, 1)

    lane8 = lax.broadcasted_iota(I32, (8, TILE), 1)
    row8 = lax.broadcasted_iota(I32, (8, TILE), 0)

    features_copy.wait()
    def columns(v, index):
        low, high = index % TILE, index // TILE
        found = jnp.zeros((8, TILE), F32)
        for t in range(OWN):
            part = pick(features[8 * v : 8 * v + 8, t * TILE : (t + 1) * TILE], low)
            found = jnp.where(high == t, part, found)
        return found

    rows_copy.wait()
    repeat = lax.broadcasted_iota(I32, (SEND, TILE), 1) % SEND == lax.broadcasted_iota(I32, (SEND, TILE), 0)
    row_list[...] = lax.dot_general(
        send_rows[...].astype(F32), repeat.astype(F32), (((0,), (0,)), ((), ())),
        precision=lax.Precision.HIGHEST, preferred_element_type=F32,
    ).astype(I32)

    group4 = lax.broadcasted_iota(I32, (4, TILE), 1) // 32
    in_group = [group4 == (t + x) % 4 for t in range(4)]

    def border_tile(q):
        lists = [jnp.broadcast_to(row_list[pl.ds(4 * q + d, 1), :], (8, TILE)) for d in range(4)]
        quarter = []
        for v in range(2):
            turned = lists[0]
            for d in range(1, 4):
                turned = jnp.where(lane8 // 32 == (d + 2 * v + row8 // 4 + x) % 4, lists[d], turned)
            found = columns(v, turned)
            quarter += [found[0:4], found[4:8]]
        for d in range(4):
            message = quarter[0]
            for a in range(4):
                message = jnp.where(in_group[(a + d) % 4], quarter[a], message)
            border_out[pl.ds(4 * q + d, 1)] = message[None]

    loop(0, BORDER, border_tile)

    for t in range(OWN):
        source[t] = features[:, t * TILE : (t + 1) * TILE]
    lane1 = lax.broadcasted_iota(I32, (1, TILE), 1)
    src_copy.wait()
    listed = jnp.zeros((1, TILE), I32)
    for k in range(SLOTS):
        listed = jnp.where(lane1 == k, tile_src[0, k], listed)
    ints[pl.ds(feat, 1)] = listed[None]

    weight_copy.wait()
    pl.semaphore_wait(barrier, N_DOM - 1 + N_FEAT - 1)

    def z_device(z_to):
        return {"dom": z_to * N_X + x}

    def x_device(x_to):
        return {"dom": z * N_X + x_to}

    def y_device(y_to):
        return {"feat": y_to * 2 + core}

    each_dom(lambda i, dx: remote(
        border_out.at[dom_far(i, dx)], border_in.at[dom], 1, {"dom": dom_far(i, dx)}).start())
    owner_copy.wait()
    hub_row_copy.wait()
    owner = hub_owner[...].reshape(1, HUBS)
    earlier = (lax.broadcasted_iota(I32, (HUBS, HUBS), 0) < lax.broadcasted_iota(I32, (HUBS, HUBS), 1))
    owned = (lax.broadcasted_iota(I32, (N_DOM, HUBS), 0) == owner).astype(F32)
    before = jnp.dot(owned.astype(BF16), earlier.astype(F32).astype(BF16), preferred_element_type=F32)
    rank = jnp.dot(jnp.ones((8, N_DOM), BF16), (owned * before).astype(BF16), preferred_element_type=F32)
    rank = rank.astype(I32)
    mine = owner == dom
    place = lax.broadcasted_iota(I32, (TILE, HUBS), 0) % 64
    chosen = (mine & (rank[0:1] == place)).astype(F32).astype(BF16)
    row = hub_row[...].reshape(1, HUBS)
    row_parts = jnp.concatenate([jnp.broadcast_to(row // 16, (8, HUBS)), jnp.broadcast_to(row % 16, (8, HUBS))], axis=0)
    my_rows = lax.dot_general(
        row_parts.astype(F32).astype(BF16), chosen, (((1,), (1,)), ((), ())), preferred_element_type=F32
    )
    my_rows = my_rows[0:8].astype(I32) * 16 + my_rows[8:16].astype(I32)

    hub_out[...] = jnp.where(lane8 < 64, columns(0, my_rows), columns(1, my_rows))

    loop(0, N_Z - 1, lambda i: remote(
        hub_out, hub_z.at[z], 0, z_device(lax.rem(z + far_first(i, N_Z), N_Z))).start())
    loop(0, N_FEAT - 1, lambda i: remote(ints.at[feat], ints.at[feat], 2, {"feat": feat_far(i)}).start())
    loop(0, N_FEAT - 1, lambda i: remote(
        source.at[feat_far(i)], picked.at[0, feat], 3, {"feat": feat_far(i)}).start())
    loop(0, N_Y - 1, lambda i: remote(
        weight_t.at[y, core], weight_t.at[y, core], 4, y_device(lax.rem(y + far_first(i, N_Y), N_Y))).start())

    picked[0, pl.ds(feat, 1)] = source[pl.ds(feat, 1)]
    border_in[pl.ds(dom, 1)] = border_out[pl.ds(dom, 1)]
    hub_z[pl.ds(z, 1)] = hub_out[...][None]

    wait_all(hub_z.at[pl.ds(0, N_Z - 1)], recv_sems.at[0])
    owner8 = jnp.broadcast_to(owner, (8, HUBS))
    at = (owner8 // N_X % 2) * 64 + rank
    pair = jnp.where(owner8 % N_X == x, owner8 // (2 * N_X), N_Z)
    found = [jnp.zeros((8, TILE), F32)] * (2 * HUB_TILES)
    for p in range(N_Z // 2):
        even, odd = hub_z[2 * p], hub_z[2 * p + 1]
        tables = (
            jnp.where(lane8 < 64, even, pltpu.roll(odd, 64, 1)),
            jnp.where(lane8 < 64, pltpu.roll(even, 64, 1), odd),
        )
        for q in range(HUB_TILES):
            span = slice(q * TILE, (q + 1) * TILE)
            for v in range(2):
                found[2 * q + v] = jnp.where(pair[:, span] == p, pick(tables[v], at[:, span]), found[2 * q + v])
    for q in range(HUB_TILES):
        for v in range(2):
            hub_part[q, 8 * v : 8 * v + 8] = found[2 * q + v]
    loop(1, N_X, lambda j: remote(hub_part, hub_x.at[x], 5, x_device(lax.rem(x + j, N_X))).start())
    hub_x[pl.ds(x, 1)] = hub_part[...][None]

    wait_all(ints.at[pl.ds(0, N_FEAT - 1)], recv_sems.at[2])
    ints_copy = pltpu.make_async_copy(ints, ints_smem, local_sems.at[2])
    ints_copy.start()

    wait_all(border_in.at[pl.ds(0, N_DOM - 1)], recv_sems.at[1])
    quarter_of = [2 * v + row8 // 4 for v in range(2)]

    def border_arrived(q):
        pieces = []
        for e in range(4):
            piece = border_in[pl.ds(4 * q + e, 1)][0]
            pieces.append(jnp.concatenate([piece, piece], axis=0))
        for v in range(2):
            mixed = pieces[0]
            for e in range(1, 4):
                mixed = jnp.where(lane8 // 32 == (quarter_of[v] + e + x) % 4, pieces[e], mixed)
            source[pl.ds(OWN + q, 1), 8 * v : 8 * v + 8] = pick(mixed, (lane8 + 32 * (quarter_of[v] + x)) % TILE)[None]

    loop(0, BORDER, border_arrived)

    ints_copy.wait()

    def send_slots(first, last, which):
        def to_peer(i):
            peer = feat_far(i)
            for k in range(first, last):
                stage[peer, k] = source[ints_smem[peer, 0, k]]
            some = pl.ds(first, last - first)
            remote(stage.at[peer, some], picked.at[some, feat], which, {"feat": peer}).start()

        loop(0, N_FEAT - 1, to_peer)
        for k in range(first, last):
            picked[k, feat] = source[tile_src[0, k]]

    send_slots(1, 2, 6)
    wait_all(hub_x.at[pl.ds(0, N_X - 1)], recv_sems.at[5])
    for q in range(HUB_TILES):
        source[OWN + BORDER + q] = (hub_x[0, q] + hub_x[1, q]) + (hub_x[2, q] + hub_x[3, q])
    send_slots(2, 4, 7)
    send_slots(4, SLOTS, 10)
    wait_all(weight_t.at[pl.ds(0, N_Y - 1), 0], recv_sems.at[4])
    other = 1 - core
    weight_on = remote(weight_t.at[:, core], weight_t.at[:, core], 12, {"feat": y * 2 + other})
    weight_on.start()

    vals_copy.wait()
    count_copy.wait()
    count = tile_count[0]
    for k in range(SLOTS):
        live = jnp.where(k < count, 1.0, 0.0).astype(F32)
        vals_high[k], vals_low[k] = split(vals[0, k] * live)

    def aggregate(first, last, which):
        wait_all(picked.at[pl.ds(first, last - first), pl.ds(0, N_FEAT - 1)], recv_sems.at[which])
        taken = [picked[k].reshape(D, TILE) for k in range(first, last)]
        taken = split(jnp.concatenate(taken, axis=1))
        rows = (last - first) * TILE
        factor = (vals_high[first:last].reshape(rows, TILE), vals_low[first:last].reshape(rows, TILE))
        return product(taken, factor, ((1,), (0,)))

    aggregated = aggregate(0, 1, 3)
    aggregated += aggregate(1, 2, 6)
    weight_on.wait_recv()
    weight_parts = split(weight_t[...].reshape(D, D))
    cot_copy.wait()
    aggregated += aggregate(2, 4, 7)
    aggregated += aggregate(4, SLOTS, 10)
    parts = split(aggregated)
    result = jnp.tanh(product(weight_parts, parts, ((1,), (0,))))
    output[...] = result
    output_copy = fetch(output, output_hbm, 9)
    pre_grad[...] = (cot[...] * (1.0 - result * result)).reshape(pre_grad.shape)

    def gradient(c, to):
        partial = product(split(pre_grad[:, c].reshape(N_Y * SHARE, TILE)), parts, ((1,), (1,)))
        for w in range(N_Y):
            for j in range(N_X):
                top, left = SHARE * w + 8 * (j // 2), TILE * (j % 2)
                to[w, j] = partial[top : top + 8, left : left + TILE]

    gradient(other, core_out)
    to_core = remote(core_out, core_in, 8, {"feat": y * 2 + other})
    to_core.start()
    gradient(core, y_out)
    to_core.wait_recv()
    y_out[...] += core_in[...]

    def to_column(i, dx):
        y_to, x_to = lax.rem(y + far_first(i, N_Y), N_Y), lax.rem(x + dx, N_X)
        device = {"dom": z * N_X + x_to, "feat": y_to * 2 + core}
        remote(y_out.at[y_to, x_to], y_in.at[y, x], 9, device).start()

    for i in range(N_Y):
        for dx in (2, 1, 3, 0):
            if (i, dx) != (N_Y - 1, 0):
                to_column(i, dx)
    y_in[pl.ds(y, 1), pl.ds(x, 1)] = y_out[pl.ds(y, 1), pl.ds(x, 1)]
    wait_most(y_in, recv_sems.at[9])
    total = [y_in[w, 0] + y_in[w, 1] + (y_in[w, 2] + y_in[w, 3]) for w in range(N_Y)]
    while len(total) > 1:
        total = [a + b for a, b in zip(total[0::2], total[1::2])]
    z_out[...] = total[0]
    loop(0, N_Z - 1, lambda i: remote(
        z_out, z_in.at[z], 11, z_device(lax.rem(z + far_first(i, N_Z), N_Z))).start())
    z_in[pl.ds(z, 1)] = z_out[...][None]
    wait_all(z_in.at[pl.ds(0, N_Z - 1)], recv_sems.at[11])
    thirds = [z_in[w] + z_in[w + 1] + (z_in[w + 2] + z_in[w + 3]) for w in range(0, N_Z, 4)]
    chunk = thirds[0] + thirds[1] + thirds[2]
    last_in[pl.ds(x, 1)] = chunk[None]
    loop(1, N_X, lambda j: remote(last_in.at[x], last_in.at[x], 13, x_device(lax.rem(x + j, N_X))).start())
    wait_all(last_in.at[pl.ds(0, N_X - 1)], recv_sems.at[13])
    whole = jnp.concatenate(
        [jnp.concatenate([last_in[0], last_in[1]], axis=1), jnp.concatenate([last_in[2], last_in[3]], axis=1)], axis=0
    )
    grad_weight[...] = whole
    fetch(grad_weight, grad_hbm, 10).wait()
    output_copy.wait()

    wait_all(hub_z.at[pl.ds(0, N_Z - 1)], send_sems.at[0])
    wait_all(border_in.at[pl.ds(0, N_DOM - 1)], send_sems.at[1])
    wait_all(ints.at[pl.ds(0, N_FEAT - 1)], send_sems.at[2])
    wait_all(picked.at[0, pl.ds(0, N_FEAT - 1)], send_sems.at[3])
    wait_all(weight_t.at[pl.ds(0, N_Y - 1), 0], send_sems.at[4])
    wait_all(hub_x.at[pl.ds(0, N_X - 1)], send_sems.at[5])
    for first, last, which in ((1, 2, 6), (2, 4, 7), (4, SLOTS, 10)):
        wait_all(picked.at[pl.ds(first, last - first), pl.ds(0, N_FEAT - 1)], send_sems.at[which])
    weight_on.wait_send()
    to_core.wait_send()
    wait_most(y_in, send_sems.at[9])
    wait_all(z_in.at[pl.ds(0, N_Z - 1)], send_sems.at[11])
    wait_all(last_in.at[pl.ds(0, N_X - 1)], send_sems.at[13])


def hand_on(output, grad_weight, output_to, grad_to, held, held_grad, sems):
    ways = ((output, held, output_to), (grad_weight, held_grad, grad_to))
    incoming = [pltpu.make_async_copy(w[0], w[1], sems.at[i]) for i, w in enumerate(ways)]
    outgoing = [pltpu.make_async_copy(w[1], w[2], sems.at[2 + i]) for i, w in enumerate(ways)]
    for copy in incoming:
        copy.start()
    for copy, onward in zip(incoming, outgoing):
        copy.wait()
        onward.start()
    for copy in outgoing:
        copy.wait()


def on_device(
    features, tile_vals, tile_src, tile_count, send_rows, hub_owner, hub_row, weight, cotangent
):
    hbm = pl.BlockSpec(memory_space=pltpu.HBM)
    scratch = [
        pltpu.VMEM(cotangent.shape, F32),
        pltpu.VMEM((SHARE, D), F32),
        pltpu.SMEM(tile_src.shape, I32),
        pltpu.SMEM(tile_count.shape, I32),
        pltpu.VMEM(features.shape, F32),
        pltpu.VMEM((SEND, N_DOM), I32),
        pltpu.VMEM((HUBS,), I32),
        pltpu.VMEM((HUBS,), I32),
        pltpu.VMEM((N_DOM, TILE), I32),
        pltpu.VMEM(tile_vals.shape, F32),
        pltpu.VMEM((SLOTS, TILE, TILE), BF16),
        pltpu.VMEM((SLOTS, TILE, TILE), BF16),
        pltpu.VMEM(cotangent.shape, F32),
        pltpu.VMEM((N_Y, 2, SHARE, TILE), F32),
        pltpu.VMEM((EXT, SHARE, TILE), F32),
        pltpu.VMEM((N_FEAT, SLOTS, SHARE, TILE), F32),
        pltpu.VMEM((SLOTS, N_FEAT, SHARE, TILE), F32),
        pltpu.VMEM((N_FEAT, 1, TILE), I32),
        pltpu.SMEM((N_FEAT, 1, TILE), I32),
        pltpu.VMEM((N_DOM, 4, TILE), F32),
        pltpu.VMEM((N_DOM, 4, TILE), F32),
        pltpu.VMEM((8, TILE), F32),
        pltpu.VMEM((N_Z, 8, TILE), F32),
        pltpu.VMEM((HUB_TILES, SHARE, TILE), F32),
        pltpu.VMEM((N_X, HUB_TILES, SHARE, TILE), F32),
        pltpu.VMEM((N_Y, 2, SHARE, D), F32),
        pltpu.VMEM((N_Y, N_X, 8, TILE), F32),
        pltpu.VMEM((N_Y, N_X, 8, TILE), F32),
        pltpu.VMEM((N_Y, N_X, 8, TILE), F32),
        pltpu.VMEM((N_Y, N_X, 8, TILE), F32),
        pltpu.VMEM((N_Y * N_X, 8, TILE), F32),
        pltpu.VMEM((8, TILE), F32),
        pltpu.VMEM((N_Z, 8, TILE), F32),
        pltpu.VMEM((N_X, 8, TILE), F32),
        pltpu.SemaphoreType.DMA((12,)),
        pltpu.SemaphoreType.DMA((14,)),
        pltpu.SemaphoreType.DMA((14,)),
    ]
    results = (
        jax.ShapeDtypeStruct(cotangent.shape, F32),
        jax.ShapeDtypeStruct((SHARE, D), F32),
    )
    made = pl.pallas_call(
        kernel,
        out_shape=results,
        in_specs=[hbm] * 9,
        out_specs=(hbm, hbm),
        scratch_shapes=scratch,
        compiler_params=pltpu.CompilerParams(
            collective_id=0, has_side_effects=True, vmem_limit_bytes=60 * 1024 * 1024
        ),
    )(
        tile_src, tile_count, features, send_rows.T, hub_owner, hub_row, weight.T, tile_vals, cotangent
    )
    output, grad_weight = pl.pallas_call(
        hand_on,
        out_shape=results,
        in_specs=[hbm, hbm],
        out_specs=(hbm, hbm),
        scratch_shapes=[pltpu.VMEM(r.shape, F32) for r in results] + [pltpu.SemaphoreType.DMA((4,))],
        compiler_params=pltpu.CompilerParams(vmem_limit_bytes=60 * 1024 * 1024),
    )(*made)
    return output, grad_weight.T


def solution(mesh):
    in_specs = (
        P("feat", "dom"),
        P(("dom", "feat"), None, None, None),
        P(("dom", "feat"), None),
        P(("dom", "feat")),
        P("dom", None),
        P(),
        P(),
        P(None, "feat"),
        P(None, ("dom", "feat")),
    )
    out_specs = (P(None, ("dom", "feat")), P(None, "feat"))
    return jax.shard_map(
        on_device, mesh=mesh, in_specs=in_specs, out_specs=out_specs, check_vma=False
    )
```

```python
import jax
import jax.numpy as jnp
from jax import lax
from jax.experimental import pallas as pl
from jax.experimental.pallas import tpu as pltpu
from jax.sharding import PartitionSpec as P

N_X, N_Z, N_Y = 4, 12, 8
N_DOM = N_X * N_Z
N_FEAT = 2 * N_Y
D = 256
TILE = 128
SHARE = D // N_FEAT
SEND = 32
SLOTS = 6
OWN = 16
BORDER = 12
HUB_TILES = 6
HUBS = HUB_TILES * TILE
EXT = OWN + BORDER + HUB_TILES
F32, BF16, I32 = jnp.float32, jnp.bfloat16, jnp.int32


def split(value):
    high = value.astype(BF16)
    return high, (value - high.astype(F32)).astype(BF16)


def product(a, b, dims):
    def one(u, v):
        return lax.dot_general(u, v, (dims, ((), ())), preferred_element_type=F32)

    return one(a[0], b[0]) + (one(a[0], b[1]) + one(a[1], b[0]))


def pick(table, index):
    return jnp.take_along_axis(table, index, axis=1, mode="promise_in_bounds")


def loop(first, last, body):
    def step(i, carry):
        body(i)
        return carry

    lax.fori_loop(first, last, step, 0)


def far_first(i, n):
    return n // 2 + (i % 2) * ((i + 1) // 2) - (1 - i % 2) * (i // 2)


def each_dom(body):
    def hops(at):
        dz = far_first(at[0], N_Z)
        return min(dz, N_Z - dz) + min(at[1], N_X - at[1])

    offsets = [(i, dx) for i in range(N_Z) for dx in (2, 1, 3, 0)][:-1]
    for i, dx in sorted(offsets, key=hops, reverse=True):
        body(i, dx)


def kernel(
    tile_src_hbm, tile_count_hbm, features_hbm, send_rows_hbm, hub_owner_hbm, hub_row_hbm, weight_hbm, tile_vals, cotangent,
    output_hbm, grad_hbm,
    output, tile_src, tile_count, features, send_rows, hub_owner, hub_row, row_list, vals, vals_high, vals_low, cot, pre_grad, source, stage, picked, ints, ints_smem,
    border_out, border_in, hub_out, hub_z, hub_part, hub_x, weight_t,
    core_out, core_in, y_out, y_in, sized, z_out, z_in, last_in,
    local_sems, send_sems, recv_sems,
):
    dom, feat = lax.axis_index("dom"), lax.axis_index("feat")
    z, x = dom // N_X, dom % N_X
    y, core = feat // 2, feat % 2

    def dom_far(i, dx):
        return lax.rem(z + far_first(i, N_Z), N_Z) * N_X + lax.rem(x + dx, N_X)

    def feat_far(i):
        t = N_FEAT - 2 - i
        j = (1 - t % 2) * (t // 2 + 1) + (t % 2) * (N_FEAT - 1 - t // 2)
        return lax.rem(feat + j, N_FEAT)

    def remote(src, dst, which, device):
        return pltpu.make_async_remote_copy(
            src_ref=src, dst_ref=dst, send_sem=send_sems.at[which], recv_sem=recv_sems.at[which],
            device_id=device, device_id_type=pl.DeviceIdType.MESH,
        )

    def wait_all(ref, sem):
        pltpu.make_async_copy(ref, ref, sem).wait()

    def wait_most(ref, sem):
        flat = sized.at[pl.ds(0, N_Y * N_X - 1)]
        wait_all(flat, sem)

    def fetch(src, dst, which):
        copy = pltpu.make_async_copy(src, dst, local_sems.at[which])
        copy.start()
        return copy

    barrier = pltpu.get_barrier_semaphore()
    each_dom(lambda i, dx: pl.semaphore_signal(
        barrier, inc=1, device_id={"dom": dom_far(i, dx)}, device_id_type=pl.DeviceIdType.MESH))
    loop(0, N_FEAT - 1, lambda i: pl.semaphore_signal(
        barrier, inc=1, device_id={"feat": feat_far(i)}, device_id_type=pl.DeviceIdType.MESH))

    src_copy = fetch(tile_src_hbm, tile_src, 11)
    owner_copy = fetch(hub_owner_hbm, hub_owner, 5)
    hub_row_copy = fetch(hub_row_hbm, hub_row, 6)
    features_copy = fetch(features_hbm, features, 3)
    rows_copy = fetch(send_rows_hbm, send_rows, 4)
    weight_copy = fetch(weight_hbm, weight_t.at[y, core], 7)
    count_copy = fetch(tile_count_hbm, tile_count, 8)
    vals_copy = fetch(tile_vals, vals, 0)
    cot_copy = fetch(cotangent, cot, 1)

    lane8 = lax.broadcasted_iota(I32, (8, TILE), 1)
    row8 = lax.broadcasted_iota(I32, (8, TILE), 0)

    features_copy.wait()
    def columns(v, index):
        low, high = index % TILE, index // TILE
        found = jnp.zeros((8, TILE), F32)
        for t in range(OWN):
            part = pick(features[8 * v : 8 * v + 8, t * TILE : (t + 1) * TILE], low)
            found = jnp.where(high == t, part, found)
        return found

    rows_copy.wait()
    repeat = lax.broadcasted_iota(I32, (SEND, TILE), 1) % SEND == lax.broadcasted_iota(I32, (SEND, TILE), 0)
    row_list[...] = lax.dot_general(
        send_rows[...].astype(F32), repeat.astype(F32), (((0,), (0,)), ((), ())),
        precision=lax.Precision.HIGHEST, preferred_element_type=F32,
    ).astype(I32)

    group4 = lax.broadcasted_iota(I32, (4, TILE), 1) // 32
    in_group = [group4 == (t + x) % 4 for t in range(4)]

    def border_tile(q):
        lists = [jnp.broadcast_to(row_list[pl.ds(4 * q + d, 1), :], (8, TILE)) for d in range(4)]
        quarter = []
        for v in range(2):
            turned = lists[0]
            for d in range(1, 4):
                turned = jnp.where(lane8 // 32 == (d + 2 * v + row8 // 4 + x) % 4, lists[d], turned)
            found = columns(v, turned)
            quarter += [found[0:4], found[4:8]]
        for d in range(4):
            message = quarter[0]
            for a in range(4):
                message = jnp.where(in_group[(a + d) % 4], quarter[a], message)
            border_out[pl.ds(4 * q + d, 1)] = message[None]

    loop(0, BORDER, border_tile)

    for t in range(OWN):
        source[t] = features[:, t * TILE : (t + 1) * TILE]
    lane1 = lax.broadcasted_iota(I32, (1, TILE), 1)
    src_copy.wait()
    listed = jnp.zeros((1, TILE), I32)
    for k in range(SLOTS):
        listed = jnp.where(lane1 == k, tile_src[0, k], listed)
    ints[pl.ds(feat, 1)] = listed[None]

    weight_copy.wait()
    pl.semaphore_wait(barrier, N_DOM - 1 + N_FEAT - 1)

    def z_device(z_to):
        return {"dom": z_to * N_X + x}

    def x_device(x_to):
        return {"dom": z * N_X + x_to}

    def y_device(y_to):
        return {"feat": y_to * 2 + core}

    each_dom(lambda i, dx: remote(
        border_out.at[dom_far(i, dx)], border_in.at[dom], 1, {"dom": dom_far(i, dx)}).start())
    owner_copy.wait()
    hub_row_copy.wait()
    owner = hub_owner[...].reshape(1, HUBS)
    earlier = (lax.broadcasted_iota(I32, (HUBS, HUBS), 0) < lax.broadcasted_iota(I32, (HUBS, HUBS), 1))
    owned = (lax.broadcasted_iota(I32, (N_DOM, HUBS), 0) == owner).astype(F32)
    before = jnp.dot(owned.astype(BF16), earlier.astype(F32).astype(BF16), preferred_element_type=F32)
    rank = jnp.dot(jnp.ones((8, N_DOM), BF16), (owned * before).astype(BF16), preferred_element_type=F32)
    rank = rank.astype(I32)
    mine = owner == dom
    place = lax.broadcasted_iota(I32, (TILE, HUBS), 0) % 64
    chosen = (mine & (rank[0:1] == place)).astype(F32).astype(BF16)
    row = hub_row[...].reshape(1, HUBS)
    row_parts = jnp.concatenate([jnp.broadcast_to(row // 16, (8, HUBS)), jnp.broadcast_to(row % 16, (8, HUBS))], axis=0)
    my_rows = lax.dot_general(
        row_parts.astype(F32).astype(BF16), chosen, (((1,), (1,)), ((), ())), preferred_element_type=F32
    )
    my_rows = my_rows[0:8].astype(I32) * 16 + my_rows[8:16].astype(I32)

    hub_out[...] = jnp.where(lane8 < 64, columns(0, my_rows), columns(1, my_rows))

    loop(0, N_Z - 1, lambda i: remote(
        hub_out, hub_z.at[z], 0, z_device(lax.rem(z + far_first(i, N_Z), N_Z))).start())
    loop(0, N_FEAT - 1, lambda i: remote(ints.at[feat], ints.at[feat], 2, {"feat": feat_far(i)}).start())
    loop(0, N_FEAT - 1, lambda i: remote(
        source.at[feat_far(i)], picked.at[0, feat], 3, {"feat": feat_far(i)}).start())
    loop(0, N_Y - 1, lambda i: remote(
        weight_t.at[y, core], weight_t.at[y, core], 4, y_device(lax.rem(y + far_first(i, N_Y), N_Y))).start())

    picked[0, pl.ds(feat, 1)] = source[pl.ds(feat, 1)]
    border_in[pl.ds(dom, 1)] = border_out[pl.ds(dom, 1)]
    hub_z[pl.ds(z, 1)] = hub_out[...][None]

    wait_all(hub_z.at[pl.ds(0, N_Z - 1)], recv_sems.at[0])
    owner8 = jnp.broadcast_to(owner, (8, HUBS))
    at = (owner8 // N_X % 2) * 64 + rank
    pair = jnp.where(owner8 % N_X == x, owner8 // (2 * N_X), N_Z)
    found = [jnp.zeros((8, TILE), F32)] * (2 * HUB_TILES)
    for p in range(N_Z // 2):
        even, odd = hub_z[2 * p], hub_z[2 * p + 1]
        tables = (
            jnp.where(lane8 < 64, even, pltpu.roll(odd, 64, 1)),
            jnp.where(lane8 < 64, pltpu.roll(even, 64, 1), odd),
        )
        for q in range(HUB_TILES):
            span = slice(q * TILE, (q + 1) * TILE)
            for v in range(2):
                found[2 * q + v] = jnp.where(pair[:, span] == p, pick(tables[v], at[:, span]), found[2 * q + v])
    for q in range(HUB_TILES):
        for v in range(2):
            hub_part[q, 8 * v : 8 * v + 8] = found[2 * q + v]
    loop(1, N_X, lambda j: remote(hub_part, hub_x.at[x], 5, x_device(lax.rem(x + j, N_X))).start())
    hub_x[pl.ds(x, 1)] = hub_part[...][None]

    wait_all(ints.at[pl.ds(0, N_FEAT - 1)], recv_sems.at[2])
    ints_copy = pltpu.make_async_copy(ints, ints_smem, local_sems.at[2])
    ints_copy.start()

    wait_all(border_in.at[pl.ds(0, N_DOM - 1)], recv_sems.at[1])
    quarter_of = [2 * v + row8 // 4 for v in range(2)]

    def border_arrived(q):
        pieces = []
        for e in range(4):
            piece = border_in[pl.ds(4 * q + e, 1)][0]
            pieces.append(jnp.concatenate([piece, piece], axis=0))
        for v in range(2):
            mixed = pieces[0]
            for e in range(1, 4):
                mixed = jnp.where(lane8 // 32 == (quarter_of[v] + e + x) % 4, pieces[e], mixed)
            source[pl.ds(OWN + q, 1), 8 * v : 8 * v + 8] = pick(mixed, (lane8 + 32 * (quarter_of[v] + x)) % TILE)[None]

    loop(0, BORDER, border_arrived)

    ints_copy.wait()

    def send_slots(first, last, which):
        def to_peer(i):
            peer = feat_far(i)
            for k in range(first, last):
                stage[peer, k] = source[ints_smem[peer, 0, k]]
            some = pl.ds(first, last - first)
            remote(stage.at[peer, some], picked.at[some, feat], which, {"feat": peer}).start()

        loop(0, N_FEAT - 1, to_peer)
        for k in range(first, last):
            picked[k, feat] = source[tile_src[0, k]]

    send_slots(1, 2, 6)
    wait_all(hub_x.at[pl.ds(0, N_X - 1)], recv_sems.at[5])
    for q in range(HUB_TILES):
        source[OWN + BORDER + q] = (hub_x[0, q] + hub_x[1, q]) + (hub_x[2, q] + hub_x[3, q])
    send_slots(2, 4, 7)
    send_slots(4, SLOTS, 10)
    wait_all(weight_t.at[pl.ds(0, N_Y - 1), 0], recv_sems.at[4])
    other = 1 - core
    weight_on = remote(weight_t.at[:, core], weight_t.at[:, core], 12, {"feat": y * 2 + other})
    weight_on.start()

    vals_copy.wait()
    count_copy.wait()
    count = tile_count[0]
    for k in range(SLOTS):
        live = jnp.where(k < count, 1.0, 0.0).astype(F32)
        vals_high[k], vals_low[k] = split(vals[0, k] * live)

    def aggregate(first, last, which):
        wait_all(picked.at[pl.ds(first, last - first), pl.ds(0, N_FEAT - 1)], recv_sems.at[which])
        taken = [picked[k].reshape(D, TILE) for k in range(first, last)]
        taken = split(jnp.concatenate(taken, axis=1))
        rows = (last - first) * TILE
        factor = (vals_high[first:last].reshape(rows, TILE), vals_low[first:last].reshape(rows, TILE))
        return product(taken, factor, ((1,), (0,)))

    aggregated = aggregate(0, 1, 3)
    aggregated += aggregate(1, 2, 6)
    weight_on.wait_recv()
    weight_parts = split(weight_t[...].reshape(D, D))
    cot_copy.wait()
    aggregated += aggregate(2, 4, 7)
    aggregated += aggregate(4, SLOTS, 10)
    parts = split(aggregated)
    result = jnp.tanh(product(weight_parts, parts, ((1,), (0,))))
    output[...] = result
    output_copy = fetch(output, output_hbm, 9)
    pre_grad[...] = (cot[...] * (1.0 - result * result)).reshape(pre_grad.shape)

    def gradient(c, to):
        partial = product(split(pre_grad[:, c].reshape(N_Y * SHARE, TILE)), parts, ((1,), (1,)))
        for w in range(N_Y):
            for j in range(N_X):
                top, left = SHARE * w + 8 * (j // 2), TILE * (j % 2)
                to[w, j] = partial[top : top + 8, left : left + TILE]

    gradient(other, core_out)
    to_core = remote(core_out, core_in, 8, {"feat": y * 2 + other})
    to_core.start()
    gradient(core, y_out)
    to_core.wait_recv()
    y_out[...] += core_in[...]

    def to_column(i, dx):
        y_to, x_to = lax.rem(y + far_first(i, N_Y), N_Y), lax.rem(x + dx, N_X)
        device = {"dom": z * N_X + x_to, "feat": y_to * 2 + core}
        remote(y_out.at[y_to, x_to], y_in.at[y, x], 9, device).start()

    for i in range(N_Y):
        for dx in (2, 1, 3, 0):
            if (i, dx) != (N_Y - 1, 0):
                to_column(i, dx)
    y_in[pl.ds(y, 1), pl.ds(x, 1)] = y_out[pl.ds(y, 1), pl.ds(x, 1)]
    wait_most(y_in, recv_sems.at[9])
    total = [y_in[w, 0] + y_in[w, 1] + (y_in[w, 2] + y_in[w, 3]) for w in range(N_Y)]
    while len(total) > 1:
        total = [a + b for a, b in zip(total[0::2], total[1::2])]
    z_out[...] = total[0]
    loop(0, N_Z - 1, lambda i: remote(
        z_out, z_in.at[z], 11, z_device(lax.rem(z + far_first(i, N_Z), N_Z))).start())
    z_in[pl.ds(z, 1)] = z_out[...][None]
    wait_all(z_in.at[pl.ds(0, N_Z - 1)], recv_sems.at[11])
    thirds = [z_in[w] + z_in[w + 1] + (z_in[w + 2] + z_in[w + 3]) for w in range(0, N_Z, 4)]
    chunk = thirds[0] + thirds[1] + thirds[2]
    last_in[pl.ds(x, 1)] = chunk[None]
    loop(1, N_X, lambda j: remote(last_in.at[x], last_in.at[x], 13, x_device(lax.rem(x + j, N_X))).start())
    wait_all(hub_z.at[pl.ds(0, N_Z - 1)], send_sems.at[0])
    wait_all(border_in.at[pl.ds(0, N_DOM - 1)], send_sems.at[1])
    wait_all(ints.at[pl.ds(0, N_FEAT - 1)], send_sems.at[2])
    wait_all(picked.at[0, pl.ds(0, N_FEAT - 1)], send_sems.at[3])
    wait_all(weight_t.at[pl.ds(0, N_Y - 1), 0], send_sems.at[4])
    wait_all(hub_x.at[pl.ds(0, N_X - 1)], send_sems.at[5])
    for first, last, which in ((1, 2, 6), (2, 4, 7), (4, SLOTS, 10)):
        wait_all(picked.at[pl.ds(first, last - first), pl.ds(0, N_FEAT - 1)], send_sems.at[which])
    weight_on.wait_send()
    to_core.wait_send()
    wait_most(y_in, send_sems.at[9])
    wait_all(z_in.at[pl.ds(0, N_Z - 1)], send_sems.at[11])
    output_copy.wait()
    wait_all(last_in.at[pl.ds(0, N_X - 1)], recv_sems.at[13])
    grad_copies = [
        fetch(last_in.at[j], grad_hbm.at[pl.ds(8 * (j // 2), 8), pl.ds(TILE * (j % 2), TILE)], (10, 12, 13, 14)[j])
        for j in range(N_X)
    ]
    wait_all(last_in.at[pl.ds(0, N_X - 1)], send_sems.at[13])
    for copy in grad_copies:
        copy.wait()


def hand_on(output, grad_weight, output_to, grad_to, held, held_grad, sems):
    ways = ((output, held, output_to), (grad_weight, held_grad, grad_to))
    incoming = [pltpu.make_async_copy(w[0], w[1], sems.at[i]) for i, w in enumerate(ways)]
    outgoing = [pltpu.make_async_copy(w[1], w[2], sems.at[2 + i]) for i, w in enumerate(ways)]
    for copy in incoming:
        copy.start()
    for copy, onward in zip(incoming, outgoing):
        copy.wait()
        onward.start()
    for copy in outgoing:
        copy.wait()


def on_device(
    features, tile_vals, tile_src, tile_count, send_rows, hub_owner, hub_row, weight, cotangent
):
    hbm = pl.BlockSpec(memory_space=pltpu.HBM)
    scratch = [
        pltpu.VMEM(cotangent.shape, F32),
        pltpu.SMEM(tile_src.shape, I32),
        pltpu.SMEM(tile_count.shape, I32),
        pltpu.VMEM(features.shape, F32),
        pltpu.VMEM((SEND, N_DOM), I32),
        pltpu.VMEM((HUBS,), I32),
        pltpu.VMEM((HUBS,), I32),
        pltpu.VMEM((N_DOM, TILE), I32),
        pltpu.VMEM(tile_vals.shape, F32),
        pltpu.VMEM((SLOTS, TILE, TILE), BF16),
        pltpu.VMEM((SLOTS, TILE, TILE), BF16),
        pltpu.VMEM(cotangent.shape, F32),
        pltpu.VMEM((N_Y, 2, SHARE, TILE), F32),
        pltpu.VMEM((EXT, SHARE, TILE), F32),
        pltpu.VMEM((N_FEAT, SLOTS, SHARE, TILE), F32),
        pltpu.VMEM((SLOTS, N_FEAT, SHARE, TILE), F32),
        pltpu.VMEM((N_FEAT, 1, TILE), I32),
        pltpu.SMEM((N_FEAT, 1, TILE), I32),
        pltpu.VMEM((N_DOM, 4, TILE), F32),
        pltpu.VMEM((N_DOM, 4, TILE), F32),
        pltpu.VMEM((8, TILE), F32),
        pltpu.VMEM((N_Z, 8, TILE), F32),
        pltpu.VMEM((HUB_TILES, SHARE, TILE), F32),
        pltpu.VMEM((N_X, HUB_TILES, SHARE, TILE), F32),
        pltpu.VMEM((N_Y, 2, SHARE, D), F32),
        pltpu.VMEM((N_Y, N_X, 8, TILE), F32),
        pltpu.VMEM((N_Y, N_X, 8, TILE), F32),
        pltpu.VMEM((N_Y, N_X, 8, TILE), F32),
        pltpu.VMEM((N_Y, N_X, 8, TILE), F32),
        pltpu.VMEM((N_Y * N_X, 8, TILE), F32),
        pltpu.VMEM((8, TILE), F32),
        pltpu.VMEM((N_Z, 8, TILE), F32),
        pltpu.VMEM((N_X, 8, TILE), F32),
        pltpu.SemaphoreType.DMA((15,)),
        pltpu.SemaphoreType.DMA((14,)),
        pltpu.SemaphoreType.DMA((14,)),
    ]
    results = (
        jax.ShapeDtypeStruct(cotangent.shape, F32),
        jax.ShapeDtypeStruct((SHARE, D), F32),
    )
    made = pl.pallas_call(
        kernel,
        out_shape=results,
        in_specs=[hbm] * 9,
        out_specs=(hbm, hbm),
        scratch_shapes=scratch,
        compiler_params=pltpu.CompilerParams(
            collective_id=0, has_side_effects=True, vmem_limit_bytes=60 * 1024 * 1024
        ),
    )(
        tile_src, tile_count, features, send_rows.T, hub_owner, hub_row, weight.T, tile_vals, cotangent
    )
    output, grad_weight = pl.pallas_call(
        hand_on,
        out_shape=results,
        in_specs=[hbm, hbm],
        out_specs=(hbm, hbm),
        scratch_shapes=[pltpu.VMEM(r.shape, F32) for r in results] + [pltpu.SemaphoreType.DMA((4,))],
        compiler_params=pltpu.CompilerParams(vmem_limit_bytes=60 * 1024 * 1024),
    )(*made)
    return output, grad_weight.T


def solution(mesh):
    in_specs = (
        P("feat", "dom"),
        P(("dom", "feat"), None, None, None),
        P(("dom", "feat"), None),
        P(("dom", "feat")),
        P("dom", None),
        P(),
        P(),
        P(None, "feat"),
        P(None, ("dom", "feat")),
    )
    out_specs = (P(None, ("dom", "feat")), P(None, "feat"))
    return jax.shard_map(
        on_device, mesh=mesh, in_specs=in_specs, out_specs=out_specs, check_vma=False
    )
```
